128 devices in a mesh: blk: 8 (over x_hi, z), grp: 16 (over y, x_lo, core).
Axes of the slice: x: 4 (x_hi: 2, x_lo: 2; x = x_hi * 2 + x_lo), y: 4, z: 4, core: 2. Of those that a mesh axis runs over, the one named last changes fastest.
Arguments:
- image_tokens: bfloat16 [512, 196, 256], P(('blk', 'grp')), may hold values from -0.375 to 0.375
- text_tokens: bfloat16 [256, 32, 256], P(('blk', 'grp')), may hold values from -0.375 to 0.375
- positives: int32 [512], P(('blk', 'grp')), may hold values from 0 to 255
Outputs:
- row_loss: float32 [512], P(('blk', 'grp'))
- grad_image: float32 [512, 196, 256], P(('blk', 'grp'))
- grad_text: float32 [256, 32, 256], P(('blk', 'grp'))
The draws below stay inside these ranges and needn't reach their ends.
All inputs are finite; a program needn't handle non-finite values.
Results may differ from the reference program's by a relative error of at most 0.0029.
Values may be sent and summed in bfloat16 or wider, within the bound.
No kernel may reach another device: no remote copies, remote signals or barrier semaphores. Data moves between devices by JAX's collectives and lax.ppermute only.
A program may use at most 64 MiB of HBM per device.

```python
import jax
import jax.numpy as jnp
from jax import lax

D = 256
IMG_TOK = 196
TXT_TOK = 32
IMAGES = 512
TEXTS = 256


def token_entries(key, total_rows, token_count):
    shape = (total_rows, token_count, D)
    entries = jnp.clip(0.0625 * jax.random.normal(key, shape, jnp.float32), -0.375, 0.375)
    return entries


def draw_image_tokens(key, part):
    key = jax.random.fold_in(key, 11)
    return token_entries(key, IMAGES, IMG_TOK).astype(jnp.bfloat16)


def draw_text_tokens(key, part):
    key = jax.random.fold_in(key, 23)
    return token_entries(key, TEXTS, TXT_TOK).astype(jnp.bfloat16)


def set_ends(array, own_key, low, largest):
    extent = array.shape
    place = [jax.random.randint(jax.random.fold_in(own_key, axis), (), 0, extent[axis]) for axis in range(len(extent))]
    array = array.at[tuple(place)].set(low)
    longest = extent.index(max(extent))
    place[longest] = (place[longest] + 1) % extent[longest]
    return array.at[tuple(place)].set(largest)


def setup_inputs(seed: int = 0) -> dict:
    streams_of = jax.random.split(jax.random.key(seed), 4)
    return {
        "image_tokens": draw_image_tokens(jax.random.fold_in(streams_of[3], 71), 0),
        "text_tokens": draw_text_tokens(jax.random.fold_in(streams_of[3], 71), 0),
        "positives": set_ends(jax.random.randint(streams_of[2], (IMAGES,), 0, TEXTS), jax.random.fold_in(streams_of[2], 1), 0, TEXTS - 1).astype(jnp.int32),
    }


SCORE_SCALE = 16.0
LOGIT_SCALE = 4.0
LOGIT_BIAS = -25.5


def reference(image_tokens, text_tokens, positives):
    text_flat = text_tokens.reshape(TEXTS * TXT_TOK, D)
    columns = jnp.arange(TEXTS, dtype=jnp.int32)

    def per_image(running, pieces):
        picture, target = pieces
        scores = SCORE_SCALE * jnp.dot(picture, text_flat.T, preferred_element_type=jnp.float32)
        score_grid = scores.reshape(IMG_TOK, TEXTS, TXT_TOK)
        row_lse = jax.nn.logsumexp(score_grid, axis=2, keepdims=True)
        col_lse = jax.nn.logsumexp(score_grid, axis=0, keepdims=True)
        similar = 0.5 * jnp.mean(row_lse[:, :, 0], axis=0) + 0.5 * jnp.mean(col_lse[0], axis=1)
        signed = jnp.where(columns == target, 1.0, -1.0).astype(jnp.float32)
        logits = LOGIT_SCALE * similar + LOGIT_BIAS
        image_loss = jnp.sum(jax.nn.softplus(-signed * logits))
        slopes = -signed * LOGIT_SCALE * jax.nn.sigmoid(-signed * logits)
        mixture = jnp.exp(score_grid - row_lse) * (0.5 / IMG_TOK) + jnp.exp(score_grid - col_lse) * (0.5 / TXT_TOK)
        weights = (SCORE_SCALE * slopes[None, :, None] * mixture).astype(jnp.bfloat16)
        weights = weights.reshape(IMG_TOK, TEXTS * TXT_TOK)
        image_grad = jnp.dot(weights, text_flat, preferred_element_type=jnp.float32)
        text_grad = jnp.dot(weights.T, picture, preferred_element_type=jnp.float32)
        return running + text_grad, (image_loss, image_grad)

    start = jnp.zeros((TEXTS * TXT_TOK, D), jnp.float32)
    summed, (row_loss, grad_image) = lax.scan(per_image, start, (image_tokens, positives))
    return row_loss, grad_image, summed.reshape(TEXTS, TXT_TOK, D)
```

```python
import functools
import jax
import jax.numpy as jnp
from jax import lax
from jax.experimental import pallas as pl
from jax.experimental.pallas import tpu as pltpu
from jax.sharding import PartitionSpec as P

SCORE_SCALE = 16.0
LOGIT_SCALE = 4.0
LOGIT_BIAS = -25.5
LOG2E = 1.4426950408889634
EXTRA = 16
CHUNK = 1024
AXES = ("blk", "grp")
CORE, X_LOW, X_HIGH = 1, 2, 64
NEIGHBOURS = (X_LOW, X_LOW | X_HIGH, X_HIGH)
CLASS = CORE | X_LOW | X_HIGH


def pair_kernel(*refs, count, chunk, img_tok, txt_tok, first, last):
    refs = list(refs)
    img_refs = [refs.pop(0) for _ in range(count)]
    txt_in, ids_ref = refs.pop(0), refs.pop(0)
    gin_ref = None if first else refs.pop(0)
    gi_refs = [refs.pop(0) for _ in range(count)]
    gt_ref = refs.pop(0)
    txt_ref = refs.pop(0) if first else txt_in
    acc_ref, it_ref, lr_ref, lc_ref, turn_ref, *more = refs
    e_refs, r_refs, c_refs = more[0:2] * count, more[2:4] * count, more[4:6] * count
    rows = img_refs[0].shape[0] - EXTRA
    cols, dim = txt_ref.shape
    texts = cols // txt_tok
    steps = cols // chunk
    tiles = chunk // 128
    groups = rows // 8

    def lanes(x):
        return [x[:, 128 * i : 128 * (i + 1)] for i in range(x.shape[1] // 128)]

    def fold_rows(x, op):
        return op(x.reshape(groups, 8, x.shape[1]), axis=0)

    def spread(x):
        return jnp.broadcast_to(x[None], (groups,) + x.shape).reshape(rows, x.shape[1])

    def over_lanes(x, op):
        shift = 64
        while shift >= texts:
            x = op(x, pltpu.roll(x, shift, 1))
            shift //= 2
        return x

    def over_rows(x, op):
        return op(x, pltpu.roll(x, 4, 0))

    def scores(img_ref, at):
        return lax.dot_general(
            img_ref[:rows], txt_ref[pl.ds(at, chunk), :], (((1,), (1,)), ((), ())), preferred_element_type=jnp.float32
        )

    def verdicts(b, row_lse_sum, col_lse_sum):
        img_ref, gi_ref = img_refs[b], gi_refs[b]
        logits = LOGIT_SCALE * (row_lse_sum * (0.5 / img_tok) + col_lse_sum * (0.5 / txt_tok)) + LOGIT_BIAS
        positives = img_ref[rows:, :128].astype(jnp.float32)[:8]
        sign = jnp.where(ids_ref[...] == positives, 1.0, -1.0).astype(jnp.float32)
        z = -sign * logits
        slope = -sign * (SCORE_SCALE * LOGIT_SCALE) / (1.0 + jnp.exp(-z))
        loss = jnp.maximum(z, 0.0) + jnp.log1p(jnp.exp(-jnp.abs(z)))
        loss = jnp.sum(loss, axis=1, keepdims=True) * (texts / 128)
        coarse = loss.astype(jnp.bfloat16).astype(jnp.float32)
        part = jnp.where(lax.broadcasted_iota(jnp.int32, (8, 1), 0) < 4, coarse, loss - coarse)
        none = jnp.zeros_like(part)
        part = jnp.concatenate([none, part] if b % 2 else [part, none], axis=0)
        gi_ref[rows:] = jnp.broadcast_to(part, (EXTRA, dim)).astype(gi_ref.dtype)
        return slope

    def weights(b, at):
        parts = []
        for i in range(tiles):
            e = e_refs[b][:, pl.ds(at + 128 * i, 128)].reshape(groups, 8, 128)
            factor = r_refs[b][...].reshape(groups, 8, 128) + c_refs[b][:, pl.ds(at + 128 * i, 128)][None]
            parts.append((e * factor).reshape(rows, 128).astype(jnp.bfloat16))
        return jnp.concatenate(parts, axis=1)

    def fast_scores(b):
        sums = []
        for j in range(steps):
            e = jnp.exp2(scores(img_refs[b], j * chunk) * (SCORE_SCALE * LOG2E))
            e_refs[b][:, j * chunk : (j + 1) * chunk] = e
            part = functools.reduce(jnp.add, lanes(e))
            if j == 0:
                r_refs[b][...] = part
            else:
                r_refs[b][...] += part
            c_refs[b][:, j * chunk : (j + 1) * chunk] = fold_rows(e, jnp.sum)

    def fast_factors(b):
        row_sum = over_lanes(r_refs[b][...], jnp.add)
        col_sum = over_rows(c_refs[b][...], jnp.add)
        low = jnp.minimum(jnp.min(fold_rows(row_sum, jnp.min)), jnp.min(col_sum))
        high = jnp.maximum(jnp.max(fold_rows(row_sum, jnp.max)), jnp.max(col_sum))
        row_lse = over_rows(fold_rows(jnp.log(row_sum), jnp.sum), jnp.add)
        col_lse = over_lanes(functools.reduce(jnp.add, lanes(jnp.log(col_sum))), jnp.add)
        slope = verdicts(b, row_lse, col_lse)
        r_refs[b][...] = spread(slope * (0.5 / img_tok)) / row_sum
        c_refs[b][...] = jnp.concatenate([slope * (0.5 / txt_tok)] * (cols // 128), axis=1) / col_sum
        return jnp.logical_and(low > 1e-30, high < 1e30)

    def fast_gradients(b):
        grad = None
        for j in range(steps):
            w = weights(b, j * chunk)
            part = jnp.dot(w, txt_ref[j * chunk : (j + 1) * chunk, :], preferred_element_type=jnp.float32)
            grad = part if grad is None else grad + part
            part = jnp.dot(it_ref[b], w, preferred_element_type=jnp.float32)
            if b == 0:
                acc_ref[:, j * chunk : (j + 1) * chunk] = part
            else:
                acc_ref[:, j * chunk : (j + 1) * chunk] += part
        gi_refs[b][:rows] = grad.astype(gi_refs[b].dtype)

    if first:
        for h, part in enumerate(lanes(txt_in[...].astype(jnp.float32))):
            turn_ref[h] = part
        for q in range(txt_tok):
            picked = [turn_ref[h, pl.ds(q, texts, stride=txt_tok), :] for h in range(dim // 128)]
            txt_ref[q * texts : (q + 1) * texts, :] = jnp.concatenate(picked, axis=1).astype(jnp.bfloat16)
    for b in range(count):
        it_ref[b] = img_refs[b][:rows].T
    fast_scores(0)
    safe = None
    for b in range(count):
        if b % 2 == 0:
            fast_scores(b + 1)
        fine = fast_factors(b)
        safe = fine if safe is None else jnp.logical_and(safe, fine)
        fast_gradients(b)
        if b % 2 == 1 and b + 1 < count:
            fast_scores(b + 1)

    def slow_block(b):
        e_ref, r_ref, c_ref = e_refs[b], r_refs[b], c_refs[b]
        r_ref[...] = jnp.full_like(r_ref, -jnp.inf)

        def tops(j, carry):
            at = pl.multiple_of(j * chunk, chunk)
            s = SCORE_SCALE * scores(img_refs[b], at)
            e_ref[:, pl.ds(at, chunk)] = s
            r_ref[...] = functools.reduce(jnp.maximum, lanes(s) + [r_ref[...]])
            c_ref[:, pl.ds(at, chunk)] = fold_rows(s, jnp.max)
            return carry

        lax.fori_loop(0, steps, tops, 0)
        r_ref[...] = over_lanes(r_ref[...], jnp.maximum)
        c_ref[...] = over_rows(c_ref[...], jnp.maximum)
        lr_ref[...] = jnp.zeros_like(lr_ref)

        def sums(j, carry):
            at = pl.multiple_of(j * chunk, chunk)
            s = e_ref[:, pl.ds(at, chunk)]
            lr_ref[...] += functools.reduce(jnp.add, [jnp.exp(x - r_ref[...]) for x in lanes(s)])
            top = spread(c_ref[:, pl.ds(at, chunk)])
            lc_ref[:, pl.ds(at, chunk)] = fold_rows(jnp.exp(s - top), jnp.sum)
            return carry

        lax.fori_loop(0, steps, sums, 0)
        lr_ref[...] = r_ref[...] + jnp.log(over_lanes(lr_ref[...], jnp.add))
        lc_ref[...] = c_ref[...] + jnp.log(over_rows(lc_ref[...], jnp.add))

        def mixtures(j, carry):
            at = pl.multiple_of(j * chunk, chunk)
            s = e_ref[:, pl.ds(at, chunk)]
            by_row = jnp.exp(s - jnp.concatenate([lr_ref[...]] * tiles, axis=1))
            by_col = jnp.exp(s - spread(lc_ref[:, pl.ds(at, chunk)]))
            e_ref[:, pl.ds(at, chunk)] = by_row * (0.5 / img_tok) + by_col * (0.5 / txt_tok)
            return carry

        lax.fori_loop(0, steps, mixtures, 0)
        row_lse = over_rows(fold_rows(lr_ref[...], jnp.sum), jnp.add)
        col_lse = over_lanes(functools.reduce(jnp.add, lanes(lc_ref[...])), jnp.add)
        slope = verdicts(b, row_lse, col_lse)
        r_ref[...] = spread(slope)
        c_ref[...] = jnp.zeros_like(c_ref)

        def gradients(j, grad):
            at = pl.multiple_of(j * chunk, chunk)
            w = weights(b, at)
            acc_ref[:, pl.ds(at, chunk)] += jnp.dot(it_ref[b], w, preferred_element_type=jnp.float32)
            return grad + jnp.dot(w, txt_ref[pl.ds(at, chunk), :], preferred_element_type=jnp.float32)

        grad = lax.fori_loop(0, steps, gradients, jnp.zeros((rows, dim), jnp.float32))
        gi_refs[b][:rows] = grad.astype(gi_refs[b].dtype)

    @pl.when(jnp.logical_not(safe))
    def _():
        acc_ref[...] = jnp.zeros_like(acc_ref)
        for b in range(count):
            slow_block(b)

    total = acc_ref[...] if first else acc_ref[...] + gin_ref[...]
    if last:
        for j in range(cols // 128):
            turned = total[:, 128 * j : 128 * (j + 1)].T
            for i in range(128 // texts):
                for h, part in enumerate(lanes(turned[i * texts : (i + 1) * texts])):
                    turn_ref[h, pl.ds(j * (128 // texts) + i, texts, stride=txt_tok), :] = part
        gt_ref[...] = jnp.concatenate([turn_ref[h] for h in range(dim // 128)], axis=1).astype(gt_ref.dtype)
    else:
        gt_ref[...] = total


def pair_call(images, texts, ids, carried, img_tok, txt_tok, last, chunk=CHUNK):
    tall, dim = images[0].shape
    count = len(images)
    rows = tall - EXTRA
    cols = texts.shape[0]
    first = carried is None
    out_shape = [jax.ShapeDtypeStruct((tall, dim), jnp.bfloat16 if b % 2 else jnp.float32) for b in range(count)]
    out_shape.append(
        jax.ShapeDtypeStruct((cols, dim), jnp.bfloat16) if last else jax.ShapeDtypeStruct((dim, cols), jnp.float32)
    )
    if first:
        out_shape.append(jax.ShapeDtypeStruct((cols, dim), jnp.bfloat16))
    scratch = [
        pltpu.VMEM((dim, cols), jnp.float32),
        pltpu.VMEM((count, dim, rows), jnp.bfloat16),
        pltpu.VMEM((rows, 128), jnp.float32),
        pltpu.VMEM((8, cols), jnp.float32),
        pltpu.VMEM((dim // 128, cols, 128), jnp.float32),
    ]
    scratch += [pltpu.VMEM((rows, cols), jnp.float32)] * 2
    scratch += [pltpu.VMEM((rows, 128), jnp.float32)] * 2
    scratch += [pltpu.VMEM((8, cols), jnp.float32)] * 2
    operands = [*images, texts, ids] + ([] if first else [carried])
    return pl.pallas_call(
        functools.partial(
            pair_kernel, count=count, chunk=chunk, img_tok=img_tok, txt_tok=txt_tok, first=first, last=last
        ),
        out_shape=out_shape,
        scratch_shapes=scratch,
        compiler_params=pltpu.CompilerParams(vmem_limit_bytes=32 * 2**20),
    )(*operands)


def body(image_tokens, text_tokens, positives):
    devices = lax.axis_size(AXES)
    own_images, img_tok, dim = image_tokens.shape
    own_texts, txt_tok, _ = text_tokens.shape
    rows = own_images * img_tok
    place = lax.axis_index("blk") * lax.axis_size("grp") + lax.axis_index("grp")
    classes = sorted({i & CLASS for i in range(devices)})
    across_texts = [[i for i in range(devices) if i & CLASS == k] for k in classes]
    peers = len(across_texts[0])

    def swapped(x, bits):
        return lax.ppermute(x, AXES, [(i, i ^ bits) for i in range(devices)])

    labels = jnp.broadcast_to(jnp.tile(positives.astype(jnp.bfloat16), EXTRA // own_images)[:, None], (EXTRA, dim))
    own = jnp.concatenate([image_tokens.transpose(1, 0, 2).reshape(rows, dim), labels], axis=0)
    text_tokens, own = lax.optimization_barrier((text_tokens, own))
    over = {bits: swapped(own, bits) for bits in NEIGHBOURS}

    sent = jnp.broadcast_to(text_tokens[None], (peers, own_texts, txt_tok, dim))
    texts = lax.all_to_all(sent, AXES, 0, 0, tiled=True, axis_index_groups=across_texts)
    X_BOTH = X_LOW | X_HIGH
    texts, over = lax.optimization_barrier((texts, over))
    over[0] = own
    beside = {bits: swapped(x, CORE) for bits, x in over.items()}
    texts = texts.reshape(peers * own_texts * txt_tok, dim)
    lane = jnp.arange(128, dtype=jnp.int32) % (peers * own_texts)
    ids = ((lane // own_texts) * 4 + (place & CLASS)) * own_texts + lane % own_texts
    ids = jnp.broadcast_to(ids.astype(jnp.float32)[None], (8, 128))

    def summed(near, met):
        return (near + met.astype(jnp.float32)).astype(jnp.bfloat16)

    found, gathered = {}, None

    def work(pairs, last=False):
        nonlocal gathered, texts
        images = [x[bits] for bits in pairs for x in (over, beside)]
        out = pair_call(images, texts, ids, gathered, img_tok, txt_tok, last)
        texts = texts if gathered is not None else out[-1]
        gathered = out[len(images)]
        for i, bits in enumerate(pairs):
            found[bits] = (out[2 * i], swapped(out[2 * i + 1], CORE))

    work([X_LOW])
    work([X_BOTH])
    *sent, gathered = lax.optimization_barrier((summed(*found[X_LOW]), summed(*found[X_BOTH]), gathered))
    back = [swapped(sent[0], X_LOW), swapped(sent[1], X_BOTH)]
    work([X_HIGH, 0], last=True)
    *back, gathered = lax.optimization_barrier((*back, gathered))
    back.append(swapped(summed(*found[X_HIGH]), X_HIGH))

    grad = found[0][0] + found[0][1].astype(jnp.float32)
    for part in back:
        grad = grad + part.astype(jnp.float32)
    grad_image = grad[:rows].reshape(img_tok, own_images, dim).transpose(1, 0, 2)
    row_loss = jnp.sum(grad[rows:, 0].reshape(EXTRA // own_images, own_images), axis=0)

    sent = gathered.reshape(peers, own_texts, txt_tok, dim)
    parts = lax.all_to_all(sent, AXES, 0, 0, tiled=True, axis_index_groups=across_texts)
    grad_text = jnp.sum(parts.astype(jnp.float32), axis=0)
    return (row_loss, grad_image, grad_text)


def solution(mesh):
    placed = (P(AXES, None, None), P(AXES, None, None), P(AXES))
    return jax.shard_map(
        body,
        mesh=mesh,
        in_specs=placed,
        out_specs=(P(AXES), P(AXES, None, None), P(AXES, None, None)),
        check_vma=False,
    )
```

```python
import functools
import jax
import jax.numpy as jnp
from jax import lax
from jax.experimental import pallas as pl
from jax.experimental.pallas import tpu as pltpu
from jax.sharding import PartitionSpec as P

SCORE_SCALE = 16.0
LOGIT_SCALE = 4.0
LOGIT_BIAS = -25.5
LOG2E = 1.4426950408889634
EXTRA = 16
CHUNK = 1024
AXES = ("blk", "grp")
CORE, X_LOW, X_HIGH = 1, 2, 64
NEIGHBOURS = (X_LOW, X_LOW | X_HIGH, X_HIGH)
CLASS = CORE | X_LOW | X_HIGH


def pair_kernel(*refs, count, chunk, img_tok, txt_tok, first, last):
    refs = list(refs)
    img_refs = [refs.pop(0) for _ in range(2 * count)]
    txt_in, ids_ref = refs.pop(0), refs.pop(0)
    gin_ref = None if first else refs.pop(0)
    gi_refs = [refs.pop(0) for _ in range(2 * count)]
    gt_ref = refs.pop(0)
    txt_ref = refs.pop(0) if first else txt_in
    acc_ref, lr_ref, lc_ref, turn_ref, *more = refs
    x_refs, xt_refs, e_refs, r_refs, c_refs = [more[count * i : count * (i + 1)] for i in range(5)]
    rows = img_refs[0].shape[0] - EXTRA
    cols, dim = txt_ref.shape
    texts = cols // txt_tok
    steps = cols // chunk
    groups = rows // 8
    every = range(0, cols, chunk)

    def lanes(x):
        return [x[:, 128 * i : 128 * (i + 1)] for i in range(x.shape[1] // 128)]

    def fold_rows(x, op):
        return op(x.reshape(2, groups, 8, x.shape[1]), axis=1)

    def spread(x):
        return jnp.broadcast_to(x[:, None], (2, groups) + x.shape[1:]).reshape(2 * rows, x.shape[2])

    def over_lanes(x, op):
        shift = 64
        while shift >= texts:
            x = op(x, pltpu.roll(x, shift, x.ndim - 1))
            shift //= 2
        return x

    def over_rows(x, op):
        return op(x, pltpu.roll(x, 4, 1))

    def over_tokens(x):
        return over_lanes(sum(x[:, :, 128 * i : 128 * (i + 1)] for i in range(cols // 128)), jnp.add)

    def scores(p, at):
        return lax.dot_general(
            x_refs[p][...], txt_ref[pl.ds(at, chunk), :], (((1,), (1,)), ((), ())), preferred_element_type=jnp.float32
        )

    def verdicts(p, row_lse_sum, col_lse_sum):
        logits = LOGIT_SCALE * (row_lse_sum * (0.5 / img_tok) + col_lse_sum * (0.5 / txt_tok)) + LOGIT_BIAS
        positives = jnp.stack([img_refs[2 * p + b][rows:, :128].astype(jnp.float32)[:8] for b in range(2)])
        sign = jnp.where(ids_ref[...][None] == positives, 1.0, -1.0).astype(jnp.float32)
        z = -sign * logits
        slope = -sign * (SCORE_SCALE * LOGIT_SCALE) / (1.0 + jnp.exp(-z))
        loss = jnp.maximum(z, 0.0) + jnp.log1p(jnp.exp(-jnp.abs(z)))
        loss = jnp.sum(loss, axis=2, keepdims=True) * (texts / 128)
        coarse = loss.astype(jnp.bfloat16).astype(jnp.float32)
        part = jnp.where(lax.broadcasted_iota(jnp.int32, (2, 8, 1), 1) < 4, coarse, loss - coarse)
        none = jnp.zeros_like(part[0])
        for b, found in enumerate(([part[0], none], [none, part[1]])):
            gi_ref = gi_refs[2 * p + b]
            gi_ref[rows:] = jnp.broadcast_to(jnp.concatenate(found, axis=0), (EXTRA, dim)).astype(gi_ref.dtype)
        return slope

    def weights(p, at, width):
        parts = []
        for i in range(width // 128):
            e = e_refs[p][:, pl.ds(at + 128 * i, 128)].reshape(2, groups, 8, 128)
            factor = r_refs[p][...].reshape(2, groups, 8, 128) + c_refs[p][:, :, pl.ds(at + 128 * i, 128)][:, None]
            parts.append((e * factor).reshape(2 * rows, 128).astype(jnp.bfloat16))
        return jnp.concatenate(parts, axis=1)

    def store_image_grad(p, grad):
        for b in range(2):
            gi_ref = gi_refs[2 * p + b]
            gi_ref[:rows] = grad[b * rows : (b + 1) * rows].astype(gi_ref.dtype)

    def fast_scores(p):
        for at in every:
            e = jnp.exp2(scores(p, at) * (SCORE_SCALE * LOG2E))
            e_refs[p][:, at : at + chunk] = e
            part = functools.reduce(jnp.add, lanes(e))
            r_refs[p][...] = part if at == 0 else r_refs[p][...] + part
            c_refs[p][:, :, at : at + chunk] = fold_rows(e, jnp.sum)

    def fast_factors(p):
        row_log = jnp.log2(over_lanes(r_refs[p][...], jnp.add))
        col_log = jnp.log2(over_rows(c_refs[p][...], jnp.add))
        low = jnp.minimum(jnp.min(fold_rows(row_log, jnp.min)), jnp.min(col_log))
        high = jnp.maximum(jnp.max(fold_rows(row_log, jnp.max)), jnp.max(col_log))
        row_lse = over_rows(fold_rows(row_log, jnp.sum), jnp.add)
        slope = verdicts(p, row_lse * (1.0 / LOG2E), over_tokens(col_log) * (1.0 / LOG2E))
        r_refs[p][...] = spread(slope * (0.5 / img_tok)) * jnp.exp2(-row_log)
        c_refs[p][...] = jnp.concatenate([slope * (0.5 / txt_tok)] * (cols // 128), axis=2) * jnp.exp2(-col_log)
        return jnp.logical_and(low > -100.0, high < 100.0)

    def fast_gradients(p):
        w = weights(p, 0, cols)
        store_image_grad(p, jnp.dot(w, txt_ref[...], preferred_element_type=jnp.float32))
        part = jnp.dot(xt_refs[p][...], w, preferred_element_type=jnp.float32)
        acc_ref[...] = part if p == 0 else acc_ref[...] + part

    def slow_pair(p):
        e_ref, r_ref, c_ref = e_refs[p], r_refs[p], c_refs[p]
        r_ref[...] = jnp.full_like(r_ref, -jnp.inf)

        def tops(j, carry):
            at = pl.multiple_of(j * chunk, chunk)
            s = SCORE_SCALE * scores(p, at)
            e_ref[:, pl.ds(at, chunk)] = s
            r_ref[...] = functools.reduce(jnp.maximum, lanes(s) + [r_ref[...]])
            c_ref[:, :, pl.ds(at, chunk)] = fold_rows(s, jnp.max)
            return carry

        lax.fori_loop(0, steps, tops, 0)
        r_ref[...] = over_lanes(r_ref[...], jnp.maximum)
        c_ref[...] = over_rows(c_ref[...], jnp.maximum)
        lr_ref[...] = jnp.zeros_like(lr_ref)

        def sums(j, carry):
            at = pl.multiple_of(j * 128, 128)
            s = e_ref[:, pl.ds(at, 128)]
            lr_ref[...] += jnp.exp(s - r_ref[...])
            lc_ref[:, :, pl.ds(at, 128)] = fold_rows(jnp.exp(s - spread(c_ref[:, :, pl.ds(at, 128)])), jnp.sum)
            return carry

        lax.fori_loop(0, cols // 128, sums, 0)
        lr_ref[...] = r_ref[...] + jnp.log(over_lanes(lr_ref[...], jnp.add))
        lc_ref[...] = c_ref[...] + jnp.log(over_rows(lc_ref[...], jnp.add))

        def mixtures(j, carry):
            at = pl.multiple_of(j * 128, 128)
            s = e_ref[:, pl.ds(at, 128)]
            by_col = jnp.exp(s - spread(lc_ref[:, :, pl.ds(at, 128)]))
            e_ref[:, pl.ds(at, 128)] = jnp.exp(s - lr_ref[...]) * (0.5 / img_tok) + by_col * (0.5 / txt_tok)
            return carry

        lax.fori_loop(0, cols // 128, mixtures, 0)
        slope = verdicts(p, over_rows(fold_rows(lr_ref[...], jnp.sum), jnp.add), over_tokens(lc_ref[...]))
        r_ref[...] = spread(slope)
        c_ref[...] = jnp.zeros_like(c_ref)

        def gradients(j, grad):
            at = pl.multiple_of(j * 256, 256)
            w = weights(p, at, 256)
            acc_ref[:, pl.ds(at, 256)] += jnp.dot(xt_refs[p][...], w, preferred_element_type=jnp.float32)
            return grad + jnp.dot(w, txt_ref[pl.ds(at, 256), :], preferred_element_type=jnp.float32)

        store_image_grad(p, lax.fori_loop(0, cols // 256, gradients, jnp.zeros((2 * rows, dim), jnp.float32)))

    if first:
        for h, part in enumerate(lanes(txt_in[...].astype(jnp.float32))):
            turn_ref[h] = part
        for q in range(txt_tok):
            picked = [turn_ref[h, pl.ds(q, texts, stride=txt_tok), :] for h in range(dim // 128)]
            txt_ref[q * texts : (q + 1) * texts, :] = jnp.concatenate(picked, axis=1).astype(jnp.bfloat16)
    for p in range(count):
        for b in range(2):
            x_refs[p][b * rows : (b + 1) * rows] = img_refs[2 * p + b][:rows]
        xt_refs[p][...] = x_refs[p][...].T
    safe = None
    for p in range(count + 1):
        if p < count:
            fast_scores(p)
        if p > 0:
            fine = fast_factors(p - 1)
            safe = fine if safe is None else jnp.logical_and(safe, fine)
            fast_gradients(p - 1)

    @pl.when(jnp.logical_not(safe))
    def _():
        acc_ref[...] = jnp.zeros_like(acc_ref)
        for p in range(count):
            slow_pair(p)

    total = acc_ref[...] if first else acc_ref[...] + gin_ref[...]
    if last:
        for j in range(cols // 128):
            turned = total[:, 128 * j : 128 * (j + 1)].T
            for i in range(128 // texts):
                for h, part in enumerate(lanes(turned[i * texts : (i + 1) * texts])):
                    turn_ref[h, pl.ds(j * (128 // texts) + i, texts, stride=txt_tok), :] = part
        gt_ref[...] = jnp.concatenate([turn_ref[h] for h in range(dim // 128)], axis=1).astype(gt_ref.dtype)
    else:
        gt_ref[...] = total


def pair_call(images, texts, ids, carried, img_tok, txt_tok, last, chunk=CHUNK):
    tall, dim = images[0].shape
    count = len(images) // 2
    rows = tall - EXTRA
    cols = texts.shape[0]
    first = carried is None
    out_shape = [jax.ShapeDtypeStruct((tall, dim), jnp.bfloat16 if b % 2 else jnp.float32) for b in range(2 * count)]
    out_shape.append(
        jax.ShapeDtypeStruct((cols, dim), jnp.bfloat16) if last else jax.ShapeDtypeStruct((dim, cols), jnp.float32)
    )
    if first:
        out_shape.append(jax.ShapeDtypeStruct((cols, dim), jnp.bfloat16))
    scratch = [
        pltpu.VMEM((dim, cols), jnp.float32),
        pltpu.VMEM((2 * rows, 128), jnp.float32),
        pltpu.VMEM((2, 8, cols), jnp.float32),
        pltpu.VMEM((dim // 128, cols, 128), jnp.float32),
    ]
    scratch += [pltpu.VMEM((2 * rows, dim), jnp.bfloat16)] * count
    scratch += [pltpu.VMEM((dim, 2 * rows), jnp.bfloat16)] * count
    scratch += [pltpu.VMEM((2 * rows, cols), jnp.float32)] * count
    scratch += [pltpu.VMEM((2 * rows, 128), jnp.float32)] * count
    scratch += [pltpu.VMEM((2, 8, cols), jnp.float32)] * count
    operands = [*images, texts, ids] + ([] if first else [carried])
    return pl.pallas_call(
        functools.partial(
            pair_kernel, count=count, chunk=chunk, img_tok=img_tok, txt_tok=txt_tok, first=first, last=last
        ),
        out_shape=out_shape,
        scratch_shapes=scratch,
        compiler_params=pltpu.CompilerParams(vmem_limit_bytes=40 * 2**20),
    )(*operands)


def body(image_tokens, text_tokens, positives):
    devices = lax.axis_size(AXES)
    own_images, img_tok, dim = image_tokens.shape
    own_texts, txt_tok, _ = text_tokens.shape
    rows = own_images * img_tok
    place = lax.axis_index("blk") * lax.axis_size("grp") + lax.axis_index("grp")
    classes = sorted({i & CLASS for i in range(devices)})
    across_texts = [[i for i in range(devices) if i & CLASS == k] for k in classes]
    peers = len(across_texts[0])

    def swapped(x, bits):
        return lax.ppermute(x, AXES, [(i, i ^ bits) for i in range(devices)])

    labels = jnp.broadcast_to(jnp.tile(positives.astype(jnp.bfloat16), EXTRA // own_images)[:, None], (EXTRA, dim))
    own = jnp.concatenate([image_tokens.transpose(1, 0, 2).reshape(rows, dim), labels], axis=0)
    text_tokens, own = lax.optimization_barrier((text_tokens, own))
    over = {bits: swapped(own, bits) for bits in NEIGHBOURS}

    sent = jnp.broadcast_to(text_tokens[None], (peers, own_texts, txt_tok, dim))
    texts = lax.all_to_all(sent, AXES, 0, 0, tiled=True, axis_index_groups=across_texts)
    X_BOTH = X_LOW | X_HIGH
    over[0] = own
    beside = {bits: swapped(x, CORE) for bits, x in over.items()}
    texts = texts.reshape(peers * own_texts * txt_tok, dim)
    lane = jnp.arange(128, dtype=jnp.int32) % (peers * own_texts)
    ids = ((lane // own_texts) * 4 + (place & CLASS)) * own_texts + lane % own_texts
    ids = jnp.broadcast_to(ids.astype(jnp.float32)[None], (8, 128))

    def summed(near, met):
        return (near + met.astype(jnp.float32)).astype(jnp.bfloat16)

    found, gathered = {}, None

    def work(pairs, last=False):
        nonlocal gathered, texts
        images = [x[bits] for bits in pairs for x in (over, beside)]
        out = pair_call(images, texts, ids, gathered, img_tok, txt_tok, last)
        texts = texts if gathered is not None else out[-1]
        gathered = out[len(images)]
        return out[: len(images)]

    near, far = work([X_LOW])
    found[X_LOW] = (near, swapped(far, CORE))
    near, far = work([X_BOTH])
    found[X_BOTH] = (near, swapped(far, CORE))
    *sent, gathered = lax.optimization_barrier((summed(*found[X_LOW]), summed(*found[X_BOTH]), gathered))
    back = [swapped(sent[0], X_LOW), swapped(sent[1], X_BOTH)]
    out = work([X_HIGH, 0], last=True)
    back, out, gathered = lax.optimization_barrier((back, out, gathered))
    found[X_HIGH] = (out[0], swapped(out[1], CORE))
    found[0] = (out[2], swapped(out[3], CORE))
    back.append(swapped(summed(*found[X_HIGH]), X_HIGH))

    grad = found[0][0] + found[0][1].astype(jnp.float32)
    for part in back:
        grad = grad + part.astype(jnp.float32)
    grad_image = grad[:rows].reshape(img_tok, own_images, dim).transpose(1, 0, 2)
    row_loss = jnp.sum(grad[rows:, 0].reshape(EXTRA // own_images, own_images), axis=0)

    sent = gathered.reshape(peers, own_texts, txt_tok, dim)
    parts = lax.all_to_all(sent, AXES, 0, 0, tiled=True, axis_index_groups=across_texts)
    grad_text = jnp.sum(parts.astype(jnp.float32), axis=0)
    return (row_loss, grad_image, grad_text)


def solution(mesh):
    placed = (P(AXES, None, None), P(AXES, None, None), P(AXES))
    return jax.shard_map(
        body,
        mesh=mesh,
        in_specs=placed,
        out_specs=(P(AXES), P(AXES, None, None), P(AXES, None, None)),
        check_vma=False,
    )
```

```python
import functools
import jax
import jax.numpy as jnp
from jax import lax
from jax.experimental import pallas as pl
from jax.experimental.pallas import tpu as pltpu
from jax.sharding import PartitionSpec as P

SCORE_SCALE = 16.0
LOGIT_SCALE = 4.0
LOGIT_BIAS = -25.5
LOG2E = 1.4426950408889634
EXTRA = 16
CHUNK = 1024
AXES = ("blk", "grp")
CORE, X_LOW, X_HIGH = 1, 2, 64
NEIGHBOURS = (X_LOW, X_LOW | X_HIGH, X_HIGH)
CLASS = CORE | X_LOW | X_HIGH


def pair_kernel(*refs, count, chunk, img_tok, txt_tok, first, last):
    refs = list(refs)
    img_refs = [refs.pop(0) for _ in range(2 * count)]
    txt_in, ids_ref = refs.pop(0), refs.pop(0)
    gin_ref = None if first else refs.pop(0)
    gi_refs = [refs.pop(0) for _ in range(2 * count)]
    gt_ref = refs.pop(0)
    txt_ref = refs.pop(0) if first else txt_in
    acc_ref, lr_ref, lc_ref, turn_ref, *more = refs
    x_refs, xt_refs, e_refs, r_refs, c_refs = [more[count * i : count * (i + 1)] for i in range(5)]
    rows = img_refs[0].shape[0] - EXTRA
    cols, dim = txt_ref.shape
    texts = cols // txt_tok
    steps = cols // chunk
    groups = rows // 8
    every = range(0, cols, chunk)

    def lanes(x):
        return [x[:, 128 * i : 128 * (i + 1)] for i in range(x.shape[1] // 128)]

    def fold_rows(x, op):
        return op(x.reshape(2, groups, 8, x.shape[1]), axis=1)

    def spread(x):
        return jnp.broadcast_to(x[:, None], (2, groups) + x.shape[1:]).reshape(2 * rows, x.shape[2])

    def over_lanes(x, op):
        shift = 64
        while shift >= texts:
            x = op(x, pltpu.roll(x, shift, x.ndim - 1))
            shift //= 2
        return x

    def over_rows(x, op):
        return op(x, pltpu.roll(x, 4, 1))

    def over_tokens(x):
        return over_lanes(sum(x[:, :, 128 * i : 128 * (i + 1)] for i in range(cols // 128)), jnp.add)

    def scores(p, at):
        return lax.dot_general(
            x_refs[p][...], txt_ref[pl.ds(at, chunk), :], (((1,), (1,)), ((), ())), preferred_element_type=jnp.float32
        )

    def verdicts(p, row_lse_sum, col_lse_sum):
        logits = LOGIT_SCALE * (row_lse_sum * (0.5 / img_tok) + col_lse_sum * (0.5 / txt_tok)) + LOGIT_BIAS
        positives = jnp.stack([img_refs[2 * p + b][rows:, :128].astype(jnp.float32)[:8] for b in range(2)])
        sign = jnp.where(ids_ref[...][None] == positives, 1.0, -1.0).astype(jnp.float32)
        z = -sign * logits
        slope = -sign * (SCORE_SCALE * LOGIT_SCALE) / (1.0 + jnp.exp(-z))
        loss = jnp.maximum(z, 0.0) + jnp.log1p(jnp.exp(-jnp.abs(z)))
        loss = jnp.sum(loss, axis=2, keepdims=True) * (texts / 128)
        coarse = loss.astype(jnp.bfloat16).astype(jnp.float32)
        part = jnp.where(lax.broadcasted_iota(jnp.int32, (2, 8, 1), 1) < 4, coarse, loss - coarse)
        none = jnp.zeros_like(part[0])
        for b, found in enumerate(([part[0], none], [none, part[1]])):
            gi_ref = gi_refs[2 * p + b]
            gi_ref[rows:] = jnp.broadcast_to(jnp.concatenate(found, axis=0), (EXTRA, dim)).astype(gi_ref.dtype)
        return slope

    def weights(p, at, width):
        parts = []
        for i in range(width // 128):
            e = e_refs[p][:, pl.ds(at + 128 * i, 128)].reshape(2, groups, 8, 128)
            factor = r_refs[p][...].reshape(2, groups, 8, 128) + c_refs[p][:, :, pl.ds(at + 128 * i, 128)][:, None]
            parts.append((e * factor).reshape(2 * rows, 128).astype(jnp.bfloat16))
        return jnp.concatenate(parts, axis=1)

    def store_image_grad(p, grad):
        for b in range(2):
            gi_ref = gi_refs[2 * p + b]
            gi_ref[:rows] = grad[b * rows : (b + 1) * rows].astype(gi_ref.dtype)

    def fast_scores(p):
        for at in every:
            e = jnp.exp2(scores(p, at) * (SCORE_SCALE * LOG2E))
            e_refs[p][:, at : at + chunk] = e
            part = functools.reduce(jnp.add, lanes(e))
            r_refs[p][...] = part if at == 0 else r_refs[p][...] + part
            c_refs[p][:, :, at : at + chunk] = fold_rows(e, jnp.sum)

    def fast_factors(p):
        row_log = jnp.log2(over_lanes(r_refs[p][...], jnp.add))
        col_log = jnp.log2(over_rows(c_refs[p][...], jnp.add))
        low = jnp.minimum(jnp.min(fold_rows(row_log, jnp.min)), jnp.min(col_log))
        high = jnp.maximum(jnp.max(fold_rows(row_log, jnp.max)), jnp.max(col_log))
        row_lse = over_rows(fold_rows(row_log, jnp.sum), jnp.add)
        slope = verdicts(p, row_lse * (1.0 / LOG2E), over_tokens(col_log) * (1.0 / LOG2E))
        r_refs[p][...] = spread(slope * (0.5 / img_tok)) * jnp.exp2(-row_log)
        c_refs[p][...] = jnp.concatenate([slope * (0.5 / txt_tok)] * (cols // 128), axis=2) * jnp.exp2(-col_log)
        return jnp.logical_and(low > -100.0, high < 100.0)

    def fast_gradients(p):
        w = weights(p, 0, cols)
        store_image_grad(p, jnp.dot(w, txt_ref[...], preferred_element_type=jnp.float32))
        part = jnp.dot(xt_refs[p][...], w, preferred_element_type=jnp.float32)
        acc_ref[...] = part if p == 0 else acc_ref[...] + part

    def slow_pair(p):
        e_ref, r_ref, c_ref = e_refs[p], r_refs[p], c_refs[p]
        r_ref[...] = jnp.full_like(r_ref, -jnp.inf)

        def tops(j, carry):
            at = pl.multiple_of(j * chunk, chunk)
            s = SCORE_SCALE * scores(p, at)
            e_ref[:, pl.ds(at, chunk)] = s
            r_ref[...] = functools.reduce(jnp.maximum, lanes(s) + [r_ref[...]])
            c_ref[:, :, pl.ds(at, chunk)] = fold_rows(s, jnp.max)
            return carry

        lax.fori_loop(0, steps, tops, 0)
        r_ref[...] = over_lanes(r_ref[...], jnp.maximum)
        c_ref[...] = over_rows(c_ref[...], jnp.maximum)
        lr_ref[...] = jnp.zeros_like(lr_ref)

        def sums(j, carry):
            at = pl.multiple_of(j * 128, 128)
            s = e_ref[:, pl.ds(at, 128)]
            lr_ref[...] += jnp.exp(s - r_ref[...])
            lc_ref[:, :, pl.ds(at, 128)] = fold_rows(jnp.exp(s - spread(c_ref[:, :, pl.ds(at, 128)])), jnp.sum)
            return carry

        lax.fori_loop(0, cols // 128, sums, 0)
        lr_ref[...] = r_ref[...] + jnp.log(over_lanes(lr_ref[...], jnp.add))
        lc_ref[...] = c_ref[...] + jnp.log(over_rows(lc_ref[...], jnp.add))

        def mixtures(j, carry):
            at = pl.multiple_of(j * 128, 128)
            s = e_ref[:, pl.ds(at, 128)]
            by_col = jnp.exp(s - spread(lc_ref[:, :, pl.ds(at, 128)]))
            e_ref[:, pl.ds(at, 128)] = jnp.exp(s - lr_ref[...]) * (0.5 / img_tok) + by_col * (0.5 / txt_tok)
            return carry

        lax.fori_loop(0, cols // 128, mixtures, 0)
        slope = verdicts(p, over_rows(fold_rows(lr_ref[...], jnp.sum), jnp.add), over_tokens(lc_ref[...]))
        r_ref[...] = spread(slope)
        c_ref[...] = jnp.zeros_like(c_ref)

        def gradients(j, grad):
            at = pl.multiple_of(j * 256, 256)
            w = weights(p, at, 256)
            acc_ref[:, pl.ds(at, 256)] += jnp.dot(xt_refs[p][...], w, preferred_element_type=jnp.float32)
            return grad + jnp.dot(w, txt_ref[pl.ds(at, 256), :], preferred_element_type=jnp.float32)

        store_image_grad(p, lax.fori_loop(0, cols // 256, gradients, jnp.zeros((2 * rows, dim), jnp.float32)))

    if first:
        for h, part in enumerate(lanes(txt_in[...].astype(jnp.float32))):
            turn_ref[h] = part
        for q in range(txt_tok):
            picked = [turn_ref[h, pl.ds(q, texts, stride=txt_tok), :] for h in range(dim // 128)]
            txt_ref[q * texts : (q + 1) * texts, :] = jnp.concatenate(picked, axis=1).astype(jnp.bfloat16)
    for p in range(count):
        for b in range(2):
            x_refs[p][b * rows : (b + 1) * rows] = img_refs[2 * p + b][:rows]
        xt_refs[p][...] = x_refs[p][...].T
    safe = None
    for p in range(count + 1):
        if p < count:
            fast_scores(p)
        if p > 0:
            fine = fast_factors(p - 1)
            safe = fine if safe is None else jnp.logical_and(safe, fine)
            fast_gradients(p - 1)

    @pl.when(jnp.logical_not(safe))
    def _():
        acc_ref[...] = jnp.zeros_like(acc_ref)
        for p in range(count):
            slow_pair(p)

    total = acc_ref[...] if first else acc_ref[...] + gin_ref[...]
    if last:
        for j in range(cols // 128):
            turned = total[:, 128 * j : 128 * (j + 1)].astype(gt_ref.dtype).T.astype(jnp.float32)
            for i in range(128 // texts):
                for h, part in enumerate(lanes(turned[i * texts : (i + 1) * texts])):
                    turn_ref[h, pl.ds(j * (128 // texts) + i, texts, stride=txt_tok), :] = part
        gt_ref[...] = jnp.concatenate([turn_ref[h] for h in range(dim // 128)], axis=1).astype(gt_ref.dtype)
    else:
        gt_ref[...] = total


def pair_call(images, texts, ids, carried, img_tok, txt_tok, last, chunk=CHUNK):
    tall, dim = images[0].shape
    count = len(images) // 2
    rows = tall - EXTRA
    cols = texts.shape[0]
    first = carried is None
    out_shape = [jax.ShapeDtypeStruct((tall, dim), jnp.bfloat16 if b % 2 else jnp.float32) for b in range(2 * count)]
    out_shape.append(
        jax.ShapeDtypeStruct((cols, dim), jnp.bfloat16) if last else jax.ShapeDtypeStruct((dim, cols), jnp.float32)
    )
    if first:
        out_shape.append(jax.ShapeDtypeStruct((cols, dim), jnp.bfloat16))
    scratch = [
        pltpu.VMEM((dim, cols), jnp.float32),
        pltpu.VMEM((2 * rows, 128), jnp.float32),
        pltpu.VMEM((2, 8, cols), jnp.float32),
        pltpu.VMEM((dim // 128, cols, 128), jnp.float32),
    ]
    scratch += [pltpu.VMEM((2 * rows, dim), jnp.bfloat16)] * count
    scratch += [pltpu.VMEM((dim, 2 * rows), jnp.bfloat16)] * count
    scratch += [pltpu.VMEM((2 * rows, cols), jnp.float32)] * count
    scratch += [pltpu.VMEM((2 * rows, 128), jnp.float32)] * count
    scratch += [pltpu.VMEM((2, 8, cols), jnp.float32)] * count
    operands = [*images, texts, ids] + ([] if first else [carried])
    return pl.pallas_call(
        functools.partial(
            pair_kernel, count=count, chunk=chunk, img_tok=img_tok, txt_tok=txt_tok, first=first, last=last
        ),
        out_shape=out_shape,
        scratch_shapes=scratch,
        compiler_params=pltpu.CompilerParams(vmem_limit_bytes=(22 + 12 * (count - 1)) * 2**20),
    )(*operands)


def body(image_tokens, text_tokens, positives):
    devices = lax.axis_size(AXES)
    own_images, img_tok, dim = image_tokens.shape
    own_texts, txt_tok, _ = text_tokens.shape
    rows = own_images * img_tok
    place = lax.axis_index("blk") * lax.axis_size("grp") + lax.axis_index("grp")
    classes = sorted({i & CLASS for i in range(devices)})
    across_texts = [[i for i in range(devices) if i & CLASS == k] for k in classes]
    peers = len(across_texts[0])

    def swapped(x, bits):
        return lax.ppermute(x, AXES, [(i, i ^ bits) for i in range(devices)])

    labels = jnp.broadcast_to(jnp.tile(positives.astype(jnp.bfloat16), EXTRA // own_images)[:, None], (EXTRA, dim))
    own = jnp.concatenate([image_tokens.transpose(1, 0, 2).reshape(rows, dim), labels], axis=0)
    over = {bits: swapped(own, bits) for bits in NEIGHBOURS}

    sent = jnp.broadcast_to(text_tokens[None], (peers, own_texts, txt_tok, dim))
    texts = lax.all_to_all(sent, AXES, 0, 0, tiled=True, axis_index_groups=across_texts)
    X_BOTH = X_LOW | X_HIGH
    over[0] = own
    beside = {bits: swapped(x, CORE) for bits, x in over.items()}
    texts = texts.reshape(peers * own_texts * txt_tok, dim)
    lane = jnp.arange(128, dtype=jnp.int32) % (peers * own_texts)
    ids = ((lane // own_texts) * 4 + (place & CLASS)) * own_texts + lane % own_texts
    ids = jnp.broadcast_to(ids.astype(jnp.float32)[None], (8, 128))

    def summed(near, met):
        return (near + met.astype(jnp.float32)).astype(jnp.bfloat16)

    found, gathered = {}, None

    def work(pairs, last=False):
        nonlocal gathered, texts
        images = [x[bits] for bits in pairs for x in (over, beside)]
        out = pair_call(images, texts, ids, gathered, img_tok, txt_tok, last)
        texts = texts if gathered is not None else out[-1]
        gathered = out[len(images)]
        return out[: len(images)]

    near, far = work([X_LOW])
    found[X_LOW] = (near, swapped(far, CORE))
    near, far = work([X_BOTH])
    found[X_BOTH] = (near, swapped(far, CORE))
    *sent, gathered = lax.optimization_barrier((summed(*found[X_LOW]), summed(*found[X_BOTH]), gathered))
    back = [swapped(sent[0], X_LOW), swapped(sent[1], X_BOTH)]
    near, far = work([X_HIGH])
    met = swapped(far, CORE)
    out = work([0], last=True)
    back, met = lax.optimization_barrier((back, met))
    found[X_HIGH] = (near, met)
    met, gathered = lax.optimization_barrier((swapped(out[1], CORE), gathered))
    found[0] = (out[0], met)
    back.append(swapped(summed(*found[X_HIGH]), X_HIGH))

    grad = found[0][0] + found[0][1].astype(jnp.float32)
    for part in back:
        grad = grad + part.astype(jnp.float32)
    grad_image = grad[:rows].reshape(img_tok, own_images, dim).transpose(1, 0, 2)
    row_loss = sum(grad[rows + n : rows + n + own_images, 0] for n in range(0, EXTRA, own_images))

    sent = gathered.reshape(peers, own_texts, txt_tok, dim)
    parts = lax.all_to_all(sent, AXES, 0, 0, tiled=True, axis_index_groups=across_texts)
    grad_text = jnp.sum(parts.astype(jnp.float32), axis=0)
    return (row_loss, grad_image, grad_text)


def solution(mesh):
    placed = (P(AXES, None, None), P(AXES, None, None), P(AXES))
    return jax.shard_map(
        body,
        mesh=mesh,
        in_specs=placed,
        out_specs=(P(AXES), P(AXES, None, None), P(AXES, None, None)),
        check_vma=False,
    )
```

```python
import functools
import jax
import jax.numpy as jnp
from jax import lax
from jax.experimental import pallas as pl
from jax.experimental.pallas import tpu as pltpu
from jax.sharding import PartitionSpec as P

SCORE_SCALE = 16.0
LOGIT_SCALE = 4.0
LOGIT_BIAS = -25.5
LOG2E = 1.4426950408889634
EXTRA = 16
CHUNK = 1024
AXES = ("blk", "grp")
CORE, X_LOW, X_HIGH = 1, 2, 64
X_BOTH = X_LOW | X_HIGH
CLASS = CORE | X_LOW | X_HIGH


def pair_kernel(*refs, count, chunk, img_tok, txt_tok, first, last):
    refs = list(refs)
    img_refs = [refs.pop(0) for _ in range(2 * count)]
    txt_in, ids_ref = refs.pop(0), refs.pop(0)
    gin_ref = None if first else refs.pop(0)
    gi_refs = [refs.pop(0) for _ in range(count)]
    far_ref = refs.pop(0)
    gi_refs = [gi_refs[b // 2] if b % 2 == 0 else far_ref.at[b // 2] for b in range(2 * count)]
    gt_ref = refs.pop(0)
    txt_ref = refs.pop(0) if first else txt_in
    acc_ref, lr_ref, lc_ref, turn_ref, *more = refs
    x_refs, xt_refs, e_refs, r_refs, c_refs = [more[count * i : count * (i + 1)] for i in range(5)]
    rows = img_refs[0].shape[0] - EXTRA
    cols, dim = txt_ref.shape
    texts = cols // txt_tok
    steps = cols // chunk
    groups = rows // 8
    every = range(0, cols, chunk)

    def lanes(x):
        return [x[:, 128 * i : 128 * (i + 1)] for i in range(x.shape[1] // 128)]

    def fold_rows(x, op):
        return op(x.reshape(2, groups, 8, x.shape[1]), axis=1)

    def spread(x):
        return jnp.broadcast_to(x[:, None], (2, groups) + x.shape[1:]).reshape(2 * rows, x.shape[2])

    def over_lanes(x, op):
        shift = 64
        while shift >= texts:
            x = op(x, pltpu.roll(x, shift, x.ndim - 1))
            shift //= 2
        return x

    def over_rows(x, op):
        return op(x, pltpu.roll(x, 4, 1))

    def over_tokens(x):
        return over_lanes(sum(x[:, :, 128 * i : 128 * (i + 1)] for i in range(cols // 128)), jnp.add)

    def scores(p, at):
        return lax.dot_general(
            x_refs[p][...], txt_ref[pl.ds(at, chunk), :], (((1,), (1,)), ((), ())), preferred_element_type=jnp.float32
        )

    def verdicts(p, row_lse_sum, col_lse_sum):
        logits = LOGIT_SCALE * (row_lse_sum * (0.5 / img_tok) + col_lse_sum * (0.5 / txt_tok)) + LOGIT_BIAS
        positives = jnp.stack([img_refs[2 * p + b][rows:, :128].astype(jnp.float32)[:8] for b in range(2)])
        sign = jnp.where(ids_ref[...][None] == positives, 1.0, -1.0).astype(jnp.float32)
        z = -sign * logits
        slope = -sign * (SCORE_SCALE * LOGIT_SCALE) / (1.0 + jnp.exp(-z))
        loss = jnp.maximum(z, 0.0) + jnp.log1p(jnp.exp(-jnp.abs(z)))
        loss = jnp.sum(loss, axis=2, keepdims=True) * (texts / 128)
        coarse = loss.astype(jnp.bfloat16).astype(jnp.float32)
        part = jnp.where(lax.broadcasted_iota(jnp.int32, (2, 8, 1), 1) < 4, coarse, loss - coarse)
        none = jnp.zeros_like(part[0])
        for b, found in enumerate(([part[0], none], [none, part[1]])):
            gi_ref = gi_refs[2 * p + b]
            gi_ref[rows:] = jnp.broadcast_to(jnp.concatenate(found, axis=0), (EXTRA, dim)).astype(gi_ref.dtype)
        return slope

    def weights(p, at, width):
        parts = []
        for i in range(width // 128):
            e = e_refs[p][:, pl.ds(at + 128 * i, 128)].reshape(2, groups, 8, 128)
            factor = r_refs[p][...].reshape(2, groups, 8, 128) + c_refs[p][:, :, pl.ds(at + 128 * i, 128)][:, None]
            parts.append((e * factor).reshape(2 * rows, 128).astype(jnp.bfloat16))
        return jnp.concatenate(parts, axis=1)

    def store_image_grad(p, grad):
        for b in range(2):
            gi_ref = gi_refs[2 * p + b]
            gi_ref[:rows] = grad[b * rows : (b + 1) * rows].astype(gi_ref.dtype)

    def fast_scores(p):
        for at in every:
            e = jnp.exp2(scores(p, at) * (SCORE_SCALE * LOG2E))
            e_refs[p][:, at : at + chunk] = e
            part = functools.reduce(jnp.add, lanes(e))
            r_refs[p][...] = part if at == 0 else r_refs[p][...] + part
            c_refs[p][:, :, at : at + chunk] = fold_rows(e, jnp.sum)

    def fast_factors(p):
        row_log = jnp.log2(over_lanes(r_refs[p][...], jnp.add))
        col_log = jnp.log2(over_rows(c_refs[p][...], jnp.add))
        low = jnp.minimum(jnp.min(fold_rows(row_log, jnp.min)), jnp.min(col_log))
        high = jnp.maximum(jnp.max(fold_rows(row_log, jnp.max)), jnp.max(col_log))
        row_lse = over_rows(fold_rows(row_log, jnp.sum), jnp.add)
        slope = verdicts(p, row_lse * (1.0 / LOG2E), over_tokens(col_log) * (1.0 / LOG2E))
        r_refs[p][...] = spread(slope * (0.5 / img_tok)) * jnp.exp2(-row_log)
        c_refs[p][...] = jnp.concatenate([slope * (0.5 / txt_tok)] * (cols // 128), axis=2) * jnp.exp2(-col_log)
        return jnp.logical_and(low > -100.0, high < 100.0)

    def fast_gradients(p):
        w = weights(p, 0, cols)
        store_image_grad(p, jnp.dot(w, txt_ref[...], preferred_element_type=jnp.float32))
        part = jnp.dot(xt_refs[p][...], w, preferred_element_type=jnp.float32)
        acc_ref[...] = part if p == 0 else acc_ref[...] + part

    def slow_pair(p):
        e_ref, r_ref, c_ref = e_refs[p], r_refs[p], c_refs[p]
        r_ref[...] = jnp.full_like(r_ref, -jnp.inf)

        def tops(j, carry):
            at = pl.multiple_of(j * chunk, chunk)
            s = SCORE_SCALE * scores(p, at)
            e_ref[:, pl.ds(at, chunk)] = s
            r_ref[...] = functools.reduce(jnp.maximum, lanes(s) + [r_ref[...]])
            c_ref[:, :, pl.ds(at, chunk)] = fold_rows(s, jnp.max)
            return carry

        lax.fori_loop(0, steps, tops, 0)
        r_ref[...] = over_lanes(r_ref[...], jnp.maximum)
        c_ref[...] = over_rows(c_ref[...], jnp.maximum)
        lr_ref[...] = jnp.zeros_like(lr_ref)

        def sums(j, carry):
            at = pl.multiple_of(j * 128, 128)
            s = e_ref[:, pl.ds(at, 128)]
            lr_ref[...] += jnp.exp(s - r_ref[...])
            lc_ref[:, :, pl.ds(at, 128)] = fold_rows(jnp.exp(s - spread(c_ref[:, :, pl.ds(at, 128)])), jnp.sum)
            return carry

        lax.fori_loop(0, cols // 128, sums, 0)
        lr_ref[...] = r_ref[...] + jnp.log(over_lanes(lr_ref[...], jnp.add))
        lc_ref[...] = c_ref[...] + jnp.log(over_rows(lc_ref[...], jnp.add))

        def mixtures(j, carry):
            at = pl.multiple_of(j * 128, 128)
            s = e_ref[:, pl.ds(at, 128)]
            by_col = jnp.exp(s - spread(lc_ref[:, :, pl.ds(at, 128)]))
            e_ref[:, pl.ds(at, 128)] = jnp.exp(s - lr_ref[...]) * (0.5 / img_tok) + by_col * (0.5 / txt_tok)
            return carry

        lax.fori_loop(0, cols // 128, mixtures, 0)
        slope = verdicts(p, over_rows(fold_rows(lr_ref[...], jnp.sum), jnp.add), over_tokens(lc_ref[...]))
        r_ref[...] = spread(slope)
        c_ref[...] = jnp.zeros_like(c_ref)

        def gradients(j, grad):
            at = pl.multiple_of(j * 256, 256)
            w = weights(p, at, 256)
            acc_ref[:, pl.ds(at, 256)] += jnp.dot(xt_refs[p][...], w, preferred_element_type=jnp.float32)
            return grad + jnp.dot(w, txt_ref[pl.ds(at, 256), :], preferred_element_type=jnp.float32)

        store_image_grad(p, lax.fori_loop(0, cols // 256, gradients, jnp.zeros((2 * rows, dim), jnp.float32)))

    if first:
        for h, part in enumerate(lanes(txt_in[...].astype(jnp.float32))):
            turn_ref[h] = part
        for q in range(txt_tok):
            picked = [turn_ref[h, pl.ds(q, texts, stride=txt_tok), :] for h in range(dim // 128)]
            txt_ref[q * texts : (q + 1) * texts, :] = jnp.concatenate(picked, axis=1).astype(jnp.bfloat16)
    for p in range(count):
        for b in range(2):
            x_refs[p][b * rows : (b + 1) * rows] = img_refs[2 * p + b][:rows]
        xt_refs[p][...] = x_refs[p][...].T
    safe = None
    for p in range(count + 1):
        if p < count:
            fast_scores(p)
        if p > 0:
            fine = fast_factors(p - 1)
            safe = fine if safe is None else jnp.logical_and(safe, fine)
            fast_gradients(p - 1)

    @pl.when(jnp.logical_not(safe))
    def _():
        acc_ref[...] = jnp.zeros_like(acc_ref)
        for p in range(count):
            slow_pair(p)

    total = acc_ref[...] if first else acc_ref[...] + gin_ref[...]
    if last:
        row = lax.broadcasted_iota(jnp.int32, (cols, 1), 0)
        source = (row % txt_tok) * texts + row // txt_tok
        pick = jnp.where(lax.broadcasted_iota(jnp.int32, (cols, cols), 1) == source, 1.0, 0.0).astype(gt_ref.dtype)
        gt_ref[...] = lax.dot_general(
            pick, total.astype(gt_ref.dtype), (((1,), (1,)), ((), ())), preferred_element_type=jnp.float32
        ).astype(gt_ref.dtype)
    else:
        gt_ref[...] = total


def pair_call(images, texts, ids, carried, img_tok, txt_tok, last, chunk=CHUNK):
    tall, dim = images[0].shape
    count = len(images) // 2
    rows = tall - EXTRA
    cols = texts.shape[0]
    first = carried is None
    out_shape = [jax.ShapeDtypeStruct((tall, dim), jnp.float32)] * count
    out_shape.append(jax.ShapeDtypeStruct((count, tall, dim), jnp.bfloat16))
    out_shape.append(
        jax.ShapeDtypeStruct((cols, dim), jnp.bfloat16) if last else jax.ShapeDtypeStruct((dim, cols), jnp.float32)
    )
    if first:
        out_shape.append(jax.ShapeDtypeStruct((cols, dim), jnp.bfloat16))
    scratch = [
        pltpu.VMEM((dim, cols), jnp.float32),
        pltpu.VMEM((2 * rows, 128), jnp.float32),
        pltpu.VMEM((2, 8, cols), jnp.float32),
        pltpu.VMEM((dim // 128, cols, 128), jnp.float32),
    ]
    scratch += [pltpu.VMEM((2 * rows, dim), jnp.bfloat16)] * count
    scratch += [pltpu.VMEM((dim, 2 * rows), jnp.bfloat16)] * count
    scratch += [pltpu.VMEM((2 * rows, cols), jnp.float32)] * count
    scratch += [pltpu.VMEM((2 * rows, 128), jnp.float32)] * count
    scratch += [pltpu.VMEM((2, 8, cols), jnp.float32)] * count
    operands = [*images, texts, ids] + ([] if first else [carried])
    return pl.pallas_call(
        functools.partial(
            pair_kernel, count=count, chunk=chunk, img_tok=img_tok, txt_tok=txt_tok, first=first, last=last
        ),
        out_shape=out_shape,
        scratch_shapes=scratch,
        compiler_params=pltpu.CompilerParams(vmem_limit_bytes=(22 + 12 * (count - 1)) * 2**20),
    )(*operands)


def body(image_tokens, text_tokens, positives):
    devices = lax.axis_size(AXES)
    own_images, img_tok, dim = image_tokens.shape
    own_texts, txt_tok, _ = text_tokens.shape
    rows = own_images * img_tok
    place = lax.axis_index("blk") * lax.axis_size("grp") + lax.axis_index("grp")
    classes = sorted({i & CLASS for i in range(devices)})
    across_texts = [[i for i in range(devices) if i & CLASS == k] for k in classes]
    peers = len(across_texts[0])

    def swapped(x, bits):
        return lax.ppermute(x, AXES, [(i, i ^ bits) for i in range(devices)])

    labels = jnp.broadcast_to(jnp.tile(positives.astype(jnp.bfloat16), EXTRA // own_images)[:, None], (EXTRA, dim))
    own = jnp.concatenate([image_tokens.transpose(1, 0, 2).reshape(rows, dim), labels], axis=0)
    over = {bits: swapped(own, bits) for bits in (X_LOW, X_BOTH)}
    over[X_HIGH] = swapped(over[X_LOW], X_BOTH)

    sent = jnp.broadcast_to(text_tokens[None], (peers, own_texts, txt_tok, dim))
    texts = lax.all_to_all(sent, AXES, 0, 0, tiled=True, axis_index_groups=across_texts)
    over[0] = own
    beside = {bits: swapped(over[bits], CORE) for bits in (X_LOW, X_BOTH, 0)}
    texts = texts.reshape(peers * own_texts * txt_tok, dim)
    lane = jnp.arange(128, dtype=jnp.int32) % (peers * own_texts)
    ids = ((lane // own_texts) * 4 + (place & CLASS)) * own_texts + lane % own_texts
    ids = jnp.broadcast_to(ids.astype(jnp.float32)[None], (8, 128))
    ids, beside[0] = lax.optimization_barrier((ids, beside[0]))

    def summed(near, met):
        return (near + met.astype(jnp.float32)).astype(jnp.bfloat16)

    def work(pairs, last=False):
        nonlocal gathered, texts
        images = [x[bits] for bits in pairs for x in (over, beside)]
        *near, far, out = pair_call(images, texts, ids, gathered, img_tok, txt_tok, last)[: len(pairs) + 2]
        gathered = out
        return near, far

    images = [x[bits] for bits in (X_LOW, X_BOTH) for x in (over, beside)]
    *near, far, gathered, texts = pair_call(images, texts, ids, None, img_tok, txt_tok, False)
    far, over[X_HIGH] = lax.optimization_barrier((far, over[X_HIGH]))
    beside[X_HIGH] = swapped(over[X_HIGH], CORE)
    met = swapped(far, CORE)
    *sent, gathered = lax.optimization_barrier((summed(near[0], met[0]), summed(near[1], met[1]), gathered))
    back = [swapped(sent[0], X_LOW), swapped(sent[1], X_BOTH)]
    (near,), far = work([X_HIGH])
    met = swapped(far, CORE)
    (own_near,), own_far = work([0], last=True)
    back, near = lax.optimization_barrier((back, near))
    own_met, gathered = lax.optimization_barrier((swapped(own_far, CORE), gathered))
    back.append(swapped(summed(near, met[0]), X_HIGH))

    grad = own_near + own_met[0].astype(jnp.float32)
    for part in back:
        grad = grad + part.astype(jnp.float32)
    grad_image = grad[:rows].reshape(img_tok, own_images, dim).transpose(1, 0, 2)
    row_loss = sum(grad[rows + n : rows + n + own_images, 0] for n in range(0, EXTRA, own_images))

    sent = gathered.reshape(peers, own_texts, txt_tok, dim)
    parts = lax.all_to_all(sent, AXES, 0, 0, tiled=True, axis_index_groups=across_texts)
    grad_text = jnp.sum(parts.astype(jnp.float32), axis=0)
    return (row_loss, grad_image, grad_text)


def solution(mesh):
    placed = (P(AXES, None, None), P(AXES, None, None), P(AXES))
    return jax.shard_map(
        body,
        mesh=mesh,
        in_specs=placed,
        out_specs=(P(AXES), P(AXES, None, None), P(AXES, None, None)),
        check_vma=False,
    )
```

```python
import functools
import jax
import jax.numpy as jnp
from jax import lax
from jax.experimental import pallas as pl
from jax.experimental.pallas import tpu as pltpu
from jax.sharding import PartitionSpec as P

SCORE_SCALE = 16.0
LOGIT_SCALE = 4.0
LOGIT_BIAS = -25.5
LOG2E = 1.4426950408889634
EXTRA = 16
CHUNK = 1024
AXES = ("blk", "grp")
CORE, X_LOW, X_HIGH = 1, 2, 64
X_BOTH = X_LOW | X_HIGH
CLASS = CORE | X_LOW | X_HIGH


def pair_kernel(*refs, count, chunk, img_tok, txt_tok, first, last):
    refs = list(refs)
    img_refs = [refs.pop(0) for _ in range(2 * count)]
    txt_in, ids_ref = refs.pop(0), refs.pop(0)
    gin_ref = None if first else refs.pop(0)
    gi_refs = [refs.pop(0) for _ in range(2 * count)]
    gi_refs = [gi_refs[b // 2 + count * (b % 2)] for b in range(2 * count)]
    gt_ref = refs.pop(0)
    txt_ref = refs.pop(0) if first else txt_in
    acc_ref, lr_ref, lc_ref, turn_ref, *more = refs
    x_refs, xt_refs, e_refs, r_refs, c_refs = [more[count * i : count * (i + 1)] for i in range(5)]
    rows = img_refs[0].shape[0] - EXTRA
    cols, dim = txt_ref.shape
    texts = cols // txt_tok
    steps = cols // chunk
    groups = rows // 8
    every = range(0, cols, chunk)

    def lanes(x):
        return [x[:, 128 * i : 128 * (i + 1)] for i in range(x.shape[1] // 128)]

    def fold_rows(x, op):
        return op(x.reshape(2, groups, 8, x.shape[1]), axis=1)

    def spread(x):
        return jnp.broadcast_to(x[:, None], (2, groups) + x.shape[1:]).reshape(2 * rows, x.shape[2])

    def over_lanes(x, op):
        shift = 64
        while shift >= texts:
            x = op(x, pltpu.roll(x, shift, x.ndim - 1))
            shift //= 2
        return x

    def over_rows(x, op):
        return op(x, pltpu.roll(x, 4, 1))

    def over_tokens(x):
        return over_lanes(sum(x[:, :, 128 * i : 128 * (i + 1)] for i in range(cols // 128)), jnp.add)

    def scores(p, at):
        return lax.dot_general(
            x_refs[p][...], txt_ref[pl.ds(at, chunk), :], (((1,), (1,)), ((), ())), preferred_element_type=jnp.float32
        )

    def verdicts(p, row_lse_sum, col_lse_sum):
        logits = LOGIT_SCALE * (row_lse_sum * (0.5 / img_tok) + col_lse_sum * (0.5 / txt_tok)) + LOGIT_BIAS
        positives = jnp.stack([img_refs[2 * p + b][rows:, :128].astype(jnp.float32)[:8] for b in range(2)])
        sign = jnp.where(ids_ref[...][None] == positives, 1.0, -1.0).astype(jnp.float32)
        z = -sign * logits
        slope = -sign * (SCORE_SCALE * LOGIT_SCALE) / (1.0 + jnp.exp(-z))
        loss = jnp.maximum(z, 0.0) + jnp.log1p(jnp.exp(-jnp.abs(z)))
        loss = jnp.sum(loss, axis=2, keepdims=True) * (texts / 128)
        coarse = loss.astype(jnp.bfloat16).astype(jnp.float32)
        part = jnp.where(lax.broadcasted_iota(jnp.int32, (2, 8, 1), 1) < 4, coarse, loss - coarse)
        none = jnp.zeros_like(part[0])
        for b, found in enumerate(([part[0], none], [none, part[1]])):
            gi_ref = gi_refs[2 * p + b]
            gi_ref[rows:] = jnp.broadcast_to(jnp.concatenate(found, axis=0), (EXTRA, dim)).astype(gi_ref.dtype)
        return slope

    def weights(p, at, width):
        parts = []
        for i in range(width // 128):
            e = e_refs[p][:, pl.ds(at + 128 * i, 128)].reshape(2, groups, 8, 128)
            factor = r_refs[p][...].reshape(2, groups, 8, 128) + c_refs[p][:, :, pl.ds(at + 128 * i, 128)][:, None]
            parts.append((e * factor).reshape(2 * rows, 128).astype(jnp.bfloat16))
        return jnp.concatenate(parts, axis=1)

    def store_image_grad(p, grad):
        for b in range(2):
            gi_ref = gi_refs[2 * p + b]
            gi_ref[:rows] = grad[b * rows : (b + 1) * rows].astype(gi_ref.dtype)

    def fast_scores(p):
        for at in every:
            e = jnp.exp2(scores(p, at) * (SCORE_SCALE * LOG2E))
            e_refs[p][:, at : at + chunk] = e
            part = functools.reduce(jnp.add, lanes(e))
            r_refs[p][...] = part if at == 0 else r_refs[p][...] + part
            c_refs[p][:, :, at : at + chunk] = fold_rows(e, jnp.sum)

    def fast_factors(p):
        row_log = jnp.log2(over_lanes(r_refs[p][...], jnp.add))
        col_log = jnp.log2(over_rows(c_refs[p][...], jnp.add))
        low = jnp.minimum(jnp.min(fold_rows(row_log, jnp.min)), jnp.min(col_log))
        high = jnp.maximum(jnp.max(fold_rows(row_log, jnp.max)), jnp.max(col_log))
        row_lse = over_rows(fold_rows(row_log, jnp.sum), jnp.add)
        slope = verdicts(p, row_lse * (1.0 / LOG2E), over_tokens(col_log) * (1.0 / LOG2E))
        r_refs[p][...] = spread(slope * (0.5 / img_tok)) * jnp.exp2(-row_log)
        c_refs[p][...] = jnp.concatenate([slope * (0.5 / txt_tok)] * (cols // 128), axis=2) * jnp.exp2(-col_log)
        return jnp.logical_and(low > -100.0, high < 100.0)

    def fast_gradients(p):
        w = weights(p, 0, cols)
        store_image_grad(p, jnp.dot(w, txt_ref[...], preferred_element_type=jnp.float32))
        part = jnp.dot(xt_refs[p][...], w, preferred_element_type=jnp.float32)
        acc_ref[...] = part if p == 0 else acc_ref[...] + part

    def slow_pair(p):
        e_ref, r_ref, c_ref = e_refs[p], r_refs[p], c_refs[p]
        r_ref[...] = jnp.full_like(r_ref, -jnp.inf)

        def tops(j, carry):
            at = pl.multiple_of(j * chunk, chunk)
            s = SCORE_SCALE * scores(p, at)
            e_ref[:, pl.ds(at, chunk)] = s
            r_ref[...] = functools.reduce(jnp.maximum, lanes(s) + [r_ref[...]])
            c_ref[:, :, pl.ds(at, chunk)] = fold_rows(s, jnp.max)
            return carry

        lax.fori_loop(0, steps, tops, 0)
        r_ref[...] = over_lanes(r_ref[...], jnp.maximum)
        c_ref[...] = over_rows(c_ref[...], jnp.maximum)
        lr_ref[...] = jnp.zeros_like(lr_ref)

        def sums(j, carry):
            at = pl.multiple_of(j * 128, 128)
            s = e_ref[:, pl.ds(at, 128)]
            lr_ref[...] += jnp.exp(s - r_ref[...])
            lc_ref[:, :, pl.ds(at, 128)] = fold_rows(jnp.exp(s - spread(c_ref[:, :, pl.ds(at, 128)])), jnp.sum)
            return carry

        lax.fori_loop(0, cols // 128, sums, 0)
        lr_ref[...] = r_ref[...] + jnp.log(over_lanes(lr_ref[...], jnp.add))
        lc_ref[...] = c_ref[...] + jnp.log(over_rows(lc_ref[...], jnp.add))

        def mixtures(j, carry):
            at = pl.multiple_of(j * 128, 128)
            s = e_ref[:, pl.ds(at, 128)]
            by_col = jnp.exp(s - spread(lc_ref[:, :, pl.ds(at, 128)]))
            e_ref[:, pl.ds(at, 128)] = jnp.exp(s - lr_ref[...]) * (0.5 / img_tok) + by_col * (0.5 / txt_tok)
            return carry

        lax.fori_loop(0, cols // 128, mixtures, 0)
        slope = verdicts(p, over_rows(fold_rows(lr_ref[...], jnp.sum), jnp.add), over_tokens(lc_ref[...]))
        r_ref[...] = spread(slope)
        c_ref[...] = jnp.zeros_like(c_ref)

        def gradients(j, grad):
            at = pl.multiple_of(j * 256, 256)
            w = weights(p, at, 256)
            acc_ref[:, pl.ds(at, 256)] += jnp.dot(xt_refs[p][...], w, preferred_element_type=jnp.float32)
            return grad + jnp.dot(w, txt_ref[pl.ds(at, 256), :], preferred_element_type=jnp.float32)

        store_image_grad(p, lax.fori_loop(0, cols // 256, gradients, jnp.zeros((2 * rows, dim), jnp.float32)))

    if first:
        for h, part in enumerate(lanes(txt_in[...].astype(jnp.float32))):
            turn_ref[h] = part
        for q in range(txt_tok):
            picked = [turn_ref[h, pl.ds(q, texts, stride=txt_tok), :] for h in range(dim // 128)]
            txt_ref[q * texts : (q + 1) * texts, :] = jnp.concatenate(picked, axis=1).astype(jnp.bfloat16)
    for p in range(count):
        for b in range(2):
            x_refs[p][b * rows : (b + 1) * rows] = img_refs[2 * p + b][:rows]
        xt_refs[p][...] = x_refs[p][...].T
    safe = None
    for p in range(count + 1):
        if p < count:
            fast_scores(p)
        if p > 0:
            fine = fast_factors(p - 1)
            safe = fine if safe is None else jnp.logical_and(safe, fine)
            fast_gradients(p - 1)

    @pl.when(jnp.logical_not(safe))
    def _():
        acc_ref[...] = jnp.zeros_like(acc_ref)
        for p in range(count):
            slow_pair(p)

    total = acc_ref[...] if first else acc_ref[...] + gin_ref[...]
    if last:
        row = lax.broadcasted_iota(jnp.int32, (cols, 1), 0)
        source = (row % txt_tok) * texts + row // txt_tok
        pick = jnp.where(lax.broadcasted_iota(jnp.int32, (cols, cols), 1) == source, 1.0, 0.0).astype(gt_ref.dtype)
        gt_ref[...] = lax.dot_general(
            pick, total.astype(gt_ref.dtype), (((1,), (1,)), ((), ())), preferred_element_type=jnp.float32
        ).astype(gt_ref.dtype)
    else:
        gt_ref[...] = total


def pair_call(images, texts, ids, carried, img_tok, txt_tok, last, chunk=CHUNK):
    tall, dim = images[0].shape
    count = len(images) // 2
    rows = tall - EXTRA
    cols = texts.shape[0]
    first = carried is None
    out_shape = [jax.ShapeDtypeStruct((tall, dim), jnp.float32)] * count
    out_shape += [jax.ShapeDtypeStruct((tall, dim), jnp.bfloat16)] * count
    out_shape.append(
        jax.ShapeDtypeStruct((cols, dim), jnp.bfloat16) if last else jax.ShapeDtypeStruct((dim, cols), jnp.float32)
    )
    if first:
        out_shape.append(jax.ShapeDtypeStruct((cols, dim), jnp.bfloat16))
    scratch = [
        pltpu.VMEM((dim, cols), jnp.float32),
        pltpu.VMEM((2 * rows, 128), jnp.float32),
        pltpu.VMEM((2, 8, cols), jnp.float32),
        pltpu.VMEM((dim // 128, cols, 128), jnp.float32),
    ]
    scratch += [pltpu.VMEM((2 * rows, dim), jnp.bfloat16)] * count
    scratch += [pltpu.VMEM((dim, 2 * rows), jnp.bfloat16)] * count
    scratch += [pltpu.VMEM((2 * rows, cols), jnp.float32)] * count
    scratch += [pltpu.VMEM((2 * rows, 128), jnp.float32)] * count
    scratch += [pltpu.VMEM((2, 8, cols), jnp.float32)] * count
    operands = [*images, texts, ids] + ([] if first else [carried])
    return pl.pallas_call(
        functools.partial(
            pair_kernel, count=count, chunk=chunk, img_tok=img_tok, txt_tok=txt_tok, first=first, last=last
        ),
        out_shape=out_shape,
        scratch_shapes=scratch,
        compiler_params=pltpu.CompilerParams(vmem_limit_bytes=(22 + 12 * (count - 1)) * 2**20),
    )(*operands)


def body(image_tokens, text_tokens, positives):
    devices = lax.axis_size(AXES)
    own_images, img_tok, dim = image_tokens.shape
    own_texts, txt_tok, _ = text_tokens.shape
    rows = own_images * img_tok
    place = lax.axis_index("blk") * lax.axis_size("grp") + lax.axis_index("grp")
    classes = sorted({i & CLASS for i in range(devices)})
    across_texts = [[i for i in range(devices) if i & CLASS == k] for k in classes]
    peers = len(across_texts[0])

    def swapped(x, bits):
        return lax.ppermute(x, AXES, [(i, i ^ bits) for i in range(devices)])

    labels = jnp.broadcast_to(jnp.tile(positives.astype(jnp.bfloat16), EXTRA // own_images)[:, None], (EXTRA, dim))
    own = jnp.concatenate([image_tokens.transpose(1, 0, 2).reshape(rows, dim), labels], axis=0)
    over = {bits: swapped(own, bits) for bits in (X_LOW, X_BOTH)}
    over[X_HIGH] = swapped(over[X_LOW], X_BOTH)

    sent = jnp.broadcast_to(text_tokens[None], (peers, own_texts, txt_tok, dim))
    texts = lax.all_to_all(sent, AXES, 0, 0, tiled=True, axis_index_groups=across_texts)
    over[0] = own
    beside = {bits: swapped(over[bits], CORE) for bits in (X_LOW, X_BOTH, 0)}
    texts = texts.reshape(peers * own_texts * txt_tok, dim)
    lane = jnp.arange(128, dtype=jnp.int32) % (peers * own_texts)
    ids = ((lane // own_texts) * 4 + (place & CLASS)) * own_texts + lane % own_texts
    ids = jnp.broadcast_to(ids.astype(jnp.float32)[None], (8, 128))
    ids, beside[0] = lax.optimization_barrier((ids, beside[0]))

    def summed(near, met):
        return (near + met.astype(jnp.float32)).astype(jnp.bfloat16)

    def work(bits, last=False):
        nonlocal gathered
        images = [over[bits], beside[bits]]
        near, far, gathered = pair_call(images, texts, ids, gathered, img_tok, txt_tok, last)
        return near, far

    images = [x[bits] for bits in (X_LOW, X_BOTH) for x in (over, beside)]
    *both, gathered, texts = pair_call(images, texts, ids, None, img_tok, txt_tok, False)
    near, far = both[:2], both[2:]
    beside[X_HIGH] = swapped(over[X_HIGH], CORE)
    met = [swapped(far[0], CORE), swapped(far[1], CORE)]
    *sent, gathered = lax.optimization_barrier((summed(near[0], met[0]), summed(near[1], met[1]), gathered))
    back = [swapped(sent[0], X_LOW), swapped(sent[1], X_BOTH)]
    near, far = work(X_HIGH)
    met = swapped(far, CORE)
    own_near, own_far = work(0, last=True)
    back, near = lax.optimization_barrier((back, near))
    own_met, gathered = lax.optimization_barrier((swapped(own_far, CORE), gathered))
    back.append(swapped(summed(near, met), X_HIGH))

    grad = own_near + own_met.astype(jnp.float32)
    for part in back:
        grad = grad + part.astype(jnp.float32)
    grad_image = grad[:rows].reshape(img_tok, own_images, dim).transpose(1, 0, 2)
    row_loss = sum(grad[rows + n : rows + n + own_images, 0] for n in range(0, EXTRA, own_images))

    sent = gathered.reshape(peers, own_texts, txt_tok, dim)
    parts = lax.all_to_all(sent, AXES, 0, 0, tiled=True, axis_index_groups=across_texts)
    grad_text = jnp.sum(parts.astype(jnp.float32), axis=0)
    return (row_loss, grad_image, grad_text)


def solution(mesh):
    placed = (P(AXES, None, None), P(AXES, None, None), P(AXES))
    return jax.shard_map(
        body,
        mesh=mesh,
        in_specs=placed,
        out_specs=(P(AXES), P(AXES, None, None), P(AXES, None, None)),
        check_vma=False,
    )
```

```python
import functools
import jax
import jax.numpy as jnp
from jax import lax
from jax.experimental import pallas as pl
from jax.experimental.pallas import tpu as pltpu
from jax.sharding import PartitionSpec as P

SCORE_SCALE = 16.0
LOGIT_SCALE = 4.0
LOGIT_BIAS = -25.5
LOG2E = 1.4426950408889634
EXTRA = 16
CHUNK = 1024
AXES = ("blk", "grp")
CORE, X_LOW, X_HIGH = 1, 2, 64
X_BOTH = X_LOW | X_HIGH
CLASS = CORE | X_LOW | X_HIGH


def pair_kernel(*refs, count, chunk, img_tok, txt_tok, first, last):
    refs = list(refs)
    img_refs = [refs.pop(0) for _ in range(2 * count)]
    txt_in, ids_ref = refs.pop(0), refs.pop(0)
    gin_ref = None if first else refs.pop(0)
    gi_refs = [refs.pop(0) for _ in range(count)]
    far_ref = refs.pop(0)
    gi_refs = [gi_refs[b // 2] if b % 2 == 0 else far_ref.at[b // 2] for b in range(2 * count)]
    gt_ref = refs.pop(0)
    txt_ref = refs.pop(0) if first else txt_in
    acc_ref, lr_ref, lc_ref, turn_ref, *more = refs
    x_refs, xt_refs, e_refs, r_refs, c_refs = [more[count * i : count * (i + 1)] for i in range(5)]
    rows = img_refs[0].shape[0] - EXTRA
    cols, dim = txt_ref.shape
    texts = cols // txt_tok
    steps = cols // chunk
    groups = rows // 8
    every = range(0, cols, chunk)

    def lanes(x):
        return [x[:, 128 * i : 128 * (i + 1)] for i in range(x.shape[1] // 128)]

    def fold_rows(x, op):
        return op(x.reshape(2, groups, 8, x.shape[1]), axis=1)

    def spread(x):
        return jnp.broadcast_to(x[:, None], (2, groups) + x.shape[1:]).reshape(2 * rows, x.shape[2])

    def over_lanes(x, op):
        shift = 64
        while shift >= texts:
            x = op(x, pltpu.roll(x, shift, x.ndim - 1))
            shift //= 2
        return x

    def over_rows(x, op):
        return op(x, pltpu.roll(x, 4, 1))

    def over_tokens(x):
        return over_lanes(sum(x[:, :, 128 * i : 128 * (i + 1)] for i in range(cols // 128)), jnp.add)

    def scores(p, at):
        return lax.dot_general(
            x_refs[p][...], txt_ref[pl.ds(at, chunk), :], (((1,), (1,)), ((), ())), preferred_element_type=jnp.float32
        )

    def verdicts(p, row_lse_sum, col_lse_sum):
        logits = LOGIT_SCALE * (row_lse_sum * (0.5 / img_tok) + col_lse_sum * (0.5 / txt_tok)) + LOGIT_BIAS
        positives = jnp.stack([img_refs[2 * p + b][rows:, :128].astype(jnp.float32)[:8] for b in range(2)])
        sign = jnp.where(ids_ref[...][None] == positives, 1.0, -1.0).astype(jnp.float32)
        z = -sign * logits
        slope = -sign * (SCORE_SCALE * LOGIT_SCALE) / (1.0 + jnp.exp(-z))
        loss = jnp.maximum(z, 0.0) + jnp.log1p(jnp.exp(-jnp.abs(z)))
        loss = jnp.sum(loss, axis=2, keepdims=True) * (texts / 128)
        coarse = loss.astype(jnp.bfloat16).astype(jnp.float32)
        part = jnp.where(lax.broadcasted_iota(jnp.int32, (2, 8, 1), 1) < 4, coarse, loss - coarse)
        none = jnp.zeros_like(part[0])
        for b, found in enumerate(([part[0], none], [none, part[1]])):
            gi_ref = gi_refs[2 * p + b]
            gi_ref[rows:] = jnp.broadcast_to(jnp.concatenate(found, axis=0), (EXTRA, dim)).astype(gi_ref.dtype)
        return slope

    def weights(p, at, width):
        parts = []
        for i in range(width // 128):
            e = e_refs[p][:, pl.ds(at + 128 * i, 128)].reshape(2, groups, 8, 128)
            factor = r_refs[p][...].reshape(2, groups, 8, 128) + c_refs[p][:, :, pl.ds(at + 128 * i, 128)][:, None]
            parts.append((e * factor).reshape(2 * rows, 128).astype(jnp.bfloat16))
        return jnp.concatenate(parts, axis=1)

    def store_image_grad(p, grad):
        for b in range(2):
            gi_ref = gi_refs[2 * p + b]
            gi_ref[:rows] = grad[b * rows : (b + 1) * rows].astype(gi_ref.dtype)

    def fast_scores(p):
        for at in every:
            e = jnp.exp2(scores(p, at) * (SCORE_SCALE * LOG2E))
            e_refs[p][:, at : at + chunk] = e
            part = functools.reduce(jnp.add, lanes(e))
            r_refs[p][...] = part if at == 0 else r_refs[p][...] + part
            c_refs[p][:, :, at : at + chunk] = fold_rows(e, jnp.sum)

    def fast_factors(p):
        row_log = jnp.log2(over_lanes(r_refs[p][...], jnp.add))
        col_log = jnp.log2(over_rows(c_refs[p][...], jnp.add))
        low = jnp.minimum(jnp.min(fold_rows(row_log, jnp.min)), jnp.min(col_log))
        high = jnp.maximum(jnp.max(fold_rows(row_log, jnp.max)), jnp.max(col_log))
        row_lse = over_rows(fold_rows(row_log, jnp.sum), jnp.add)
        slope = verdicts(p, row_lse * (1.0 / LOG2E), over_tokens(col_log) * (1.0 / LOG2E))
        r_refs[p][...] = spread(slope * (0.5 / img_tok)) * jnp.exp2(-row_log)
        c_refs[p][...] = jnp.concatenate([slope * (0.5 / txt_tok)] * (cols // 128), axis=2) * jnp.exp2(-col_log)
        return jnp.logical_and(low > -100.0, high < 100.0)

    def fast_gradients(p):
        grad = None
        for at in range(0, cols, 256):
            w = weights(p, at, 256)
            part = jnp.dot(w, txt_ref[at : at + 256, :], preferred_element_type=jnp.float32)
            grad = part if grad is None else grad + part
            part = jnp.dot(xt_refs[p][...], w, preferred_element_type=jnp.float32)
            acc_ref[:, at : at + 256] = part if p == 0 else acc_ref[:, at : at + 256] + part
        store_image_grad(p, grad)

    def slow_pair(p):
        e_ref, r_ref, c_ref = e_refs[p], r_refs[p], c_refs[p]
        r_ref[...] = jnp.full_like(r_ref, -jnp.inf)

        def tops(j, carry):
            at = pl.multiple_of(j * chunk, chunk)
            s = SCORE_SCALE * scores(p, at)
            e_ref[:, pl.ds(at, chunk)] = s
            r_ref[...] = functools.reduce(jnp.maximum, lanes(s) + [r_ref[...]])
            c_ref[:, :, pl.ds(at, chunk)] = fold_rows(s, jnp.max)
            return carry

        lax.fori_loop(0, steps, tops, 0)
        r_ref[...] = over_lanes(r_ref[...], jnp.maximum)
        c_ref[...] = over_rows(c_ref[...], jnp.maximum)
        lr_ref[...] = jnp.zeros_like(lr_ref)

        def sums(j, carry):
            at = pl.multiple_of(j * 128, 128)
            s = e_ref[:, pl.ds(at, 128)]
            lr_ref[...] += jnp.exp(s - r_ref[...])
            lc_ref[:, :, pl.ds(at, 128)] = fold_rows(jnp.exp(s - spread(c_ref[:, :, pl.ds(at, 128)])), jnp.sum)
            return carry

        lax.fori_loop(0, cols // 128, sums, 0)
        lr_ref[...] = r_ref[...] + jnp.log(over_lanes(lr_ref[...], jnp.add))
        lc_ref[...] = c_ref[...] + jnp.log(over_rows(lc_ref[...], jnp.add))

        def mixtures(j, carry):
            at = pl.multiple_of(j * 128, 128)
            s = e_ref[:, pl.ds(at, 128)]
            by_col = jnp.exp(s - spread(lc_ref[:, :, pl.ds(at, 128)]))
            e_ref[:, pl.ds(at, 128)] = jnp.exp(s - lr_ref[...]) * (0.5 / img_tok) + by_col * (0.5 / txt_tok)
            return carry

        lax.fori_loop(0, cols // 128, mixtures, 0)
        slope = verdicts(p, over_rows(fold_rows(lr_ref[...], jnp.sum), jnp.add), over_tokens(lc_ref[...]))
        r_ref[...] = spread(slope)
        c_ref[...] = jnp.zeros_like(c_ref)

        def gradients(j, grad):
            at = pl.multiple_of(j * 256, 256)
            w = weights(p, at, 256)
            acc_ref[:, pl.ds(at, 256)] += jnp.dot(xt_refs[p][...], w, preferred_element_type=jnp.float32)
            return grad + jnp.dot(w, txt_ref[pl.ds(at, 256), :], preferred_element_type=jnp.float32)

        store_image_grad(p, lax.fori_loop(0, cols // 256, gradients, jnp.zeros((2 * rows, dim), jnp.float32)))

    if first:
        for h, part in enumerate(lanes(txt_in[...].astype(jnp.float32))):
            turn_ref[h] = part
        for q in range(txt_tok):
            picked = [turn_ref[h, pl.ds(q, texts, stride=txt_tok), :] for h in range(dim // 128)]
            txt_ref[q * texts : (q + 1) * texts, :] = jnp.concatenate(picked, axis=1).astype(jnp.bfloat16)
    for p in range(count):
        for b in range(2):
            x_refs[p][b * rows : (b + 1) * rows] = img_refs[2 * p + b][:rows]
        xt_refs[p][...] = x_refs[p][...].T
    safe = None
    for p in range(count + 1):
        if p < count:
            fast_scores(p)
        if p > 0:
            fine = fast_factors(p - 1)
            safe = fine if safe is None else jnp.logical_and(safe, fine)
            fast_gradients(p - 1)

    @pl.when(jnp.logical_not(safe))
    def _():
        acc_ref[...] = jnp.zeros_like(acc_ref)
        for p in range(count):
            slow_pair(p)

    total = acc_ref[...] if first else acc_ref[...] + gin_ref[...]
    if last:
        row = lax.broadcasted_iota(jnp.int32, (cols, 1), 0)
        source = (row % txt_tok) * texts + row // txt_tok
        pick = jnp.where(lax.broadcasted_iota(jnp.int32, (cols, cols), 1) == source, 1.0, 0.0).astype(gt_ref.dtype)
        gt_ref[...] = lax.dot_general(
            pick, total.astype(gt_ref.dtype), (((1,), (1,)), ((), ())), preferred_element_type=jnp.float32
        ).astype(gt_ref.dtype)
    else:
        gt_ref[...] = total


def pair_call(images, texts, ids, carried, img_tok, txt_tok, last, chunk=CHUNK):
    tall, dim = images[0].shape
    count = len(images) // 2
    rows = tall - EXTRA
    cols = texts.shape[0]
    first = carried is None
    out_shape = [jax.ShapeDtypeStruct((tall, dim), jnp.float32)] * count
    out_shape.append(jax.ShapeDtypeStruct((count, tall, dim), jnp.bfloat16))
    out_shape.append(
        jax.ShapeDtypeStruct((cols, dim), jnp.bfloat16) if last else jax.ShapeDtypeStruct((dim, cols), jnp.float32)
    )
    if first:
        out_shape.append(jax.ShapeDtypeStruct((cols, dim), jnp.bfloat16))
    scratch = [
        pltpu.VMEM((dim, cols), jnp.float32),
        pltpu.VMEM((2 * rows, 128), jnp.float32),
        pltpu.VMEM((2, 8, cols), jnp.float32),
        pltpu.VMEM((dim // 128, cols, 128), jnp.float32),
    ]
    scratch += [pltpu.VMEM((2 * rows, dim), jnp.bfloat16)] * count
    scratch += [pltpu.VMEM((dim, 2 * rows), jnp.bfloat16)] * count
    scratch += [pltpu.VMEM((2 * rows, cols), jnp.float32)] * count
    scratch += [pltpu.VMEM((2 * rows, 128), jnp.float32)] * count
    scratch += [pltpu.VMEM((2, 8, cols), jnp.float32)] * count
    operands = [*images, texts, ids] + ([] if first else [carried])
    return pl.pallas_call(
        functools.partial(
            pair_kernel, count=count, chunk=chunk, img_tok=img_tok, txt_tok=txt_tok, first=first, last=last
        ),
        out_shape=out_shape,
        scratch_shapes=scratch,
        compiler_params=pltpu.CompilerParams(vmem_limit_bytes=(22 + 12 * (count - 1)) * 2**20),
    )(*operands)


def body(image_tokens, text_tokens, positives):
    devices = lax.axis_size(AXES)
    own_images, img_tok, dim = image_tokens.shape
    own_texts, txt_tok, _ = text_tokens.shape
    rows = own_images * img_tok
    place = lax.axis_index("blk") * lax.axis_size("grp") + lax.axis_index("grp")
    classes = sorted({i & CLASS for i in range(devices)})
    across_texts = [[i for i in range(devices) if i & CLASS == k] for k in classes]
    peers = len(across_texts[0])

    def swapped(x, bits):
        return lax.ppermute(x, AXES, [(i, i ^ bits) for i in range(devices)])

    labels = jnp.broadcast_to(jnp.tile(positives.astype(jnp.bfloat16), EXTRA // own_images)[:, None], (EXTRA, dim))
    own = jnp.concatenate([image_tokens.transpose(1, 0, 2).reshape(rows, dim), labels], axis=0)
    over = {bits: swapped(own, bits) for bits in (X_LOW, X_BOTH)}
    over[X_HIGH] = swapped(over[X_LOW], X_BOTH)

    sent = jnp.broadcast_to(text_tokens[None], (peers, own_texts, txt_tok, dim))
    texts = lax.all_to_all(sent, AXES, 0, 0, tiled=True, axis_index_groups=across_texts)
    over[0] = own
    beside = {bits: swapped(over[bits], CORE) for bits in (X_LOW, X_BOTH, 0)}
    texts = texts.reshape(peers * own_texts * txt_tok, dim)
    lane = jnp.arange(128, dtype=jnp.int32) % (peers * own_texts)
    ids = ((lane // own_texts) * 4 + (place & CLASS)) * own_texts + lane % own_texts
    ids = jnp.broadcast_to(ids.astype(jnp.float32)[None], (8, 128))
    ids, beside[0] = lax.optimization_barrier((ids, beside[0]))

    def summed(near, met):
        return (near + met.astype(jnp.float32)).astype(jnp.bfloat16)

    def work(pairs, last=False):
        nonlocal gathered, texts
        images = [x[bits] for bits in pairs for x in (over, beside)]
        *near, far, out = pair_call(images, texts, ids, gathered, img_tok, txt_tok, last)[: len(pairs) + 2]
        gathered = out
        return near, far

    images = [x[bits] for bits in (X_LOW, X_BOTH) for x in (over, beside)]
    *near, far, gathered, texts = pair_call(images, texts, ids, None, img_tok, txt_tok, False)
    far, over[X_HIGH] = lax.optimization_barrier((far, over[X_HIGH]))
    beside[X_HIGH] = swapped(over[X_HIGH], CORE)
    met = swapped(far, CORE)
    *sent, gathered = lax.optimization_barrier((summed(near[0], met[0]), summed(near[1], met[1]), gathered))
    back = [swapped(sent[0], X_LOW), swapped(sent[1], X_BOTH)]
    (near,), far = work([X_HIGH])
    met = swapped(far, CORE)
    (own_near,), own_far = work([0], last=True)
    back, near = lax.optimization_barrier((back, near))
    own_met, gathered = lax.optimization_barrier((swapped(own_far, CORE), gathered))
    back.append(swapped(summed(near, met[0]), X_HIGH))

    grad = own_near + own_met[0].astype(jnp.float32)
    for part in back:
        grad = grad + part.astype(jnp.float32)
    grad_image = grad[:rows].reshape(img_tok, own_images, dim).transpose(1, 0, 2)
    row_loss = sum(grad[rows + n : rows + n + own_images, 0] for n in range(0, EXTRA, own_images))

    sent = gathered.reshape(peers, own_texts, txt_tok, dim)
    parts = lax.all_to_all(sent, AXES, 0, 0, tiled=True, axis_index_groups=across_texts)
    grad_text = jnp.sum(parts.astype(jnp.float32), axis=0)
    return (row_loss, grad_image, grad_text)


def solution(mesh):
    placed = (P(AXES, None, None), P(AXES, None, None), P(AXES))
    return jax.shard_map(
        body,
        mesh=mesh,
        in_specs=placed,
        out_specs=(P(AXES), P(AXES, None, None), P(AXES, None, None)),
        check_vma=False,
    )
```

```python
import functools
import jax
import jax.numpy as jnp
from jax import lax
from jax.experimental import pallas as pl
from jax.experimental.pallas import tpu as pltpu
from jax.sharding import PartitionSpec as P

SCORE_SCALE = 16.0
LOGIT_SCALE = 4.0
LOGIT_BIAS = -25.5
LOG2E = 1.4426950408889634
EXTRA = 16
CHUNK = 1024
AXES = ("blk", "grp")
CORE, X_LOW, X_HIGH = 1, 2, 64
CLASS = CORE | X_LOW | X_HIGH


def pair_kernel(*refs, count, chunk, img_tok, txt_tok, first, last):
    refs = list(refs)
    img_refs = [refs.pop(0) for _ in range(2 * count)]
    txt_in, ids_ref = refs.pop(0), refs.pop(0)
    gin_ref = None if first else refs.pop(0)
    gi_refs = [refs.pop(0) for _ in range(2 * count)]
    gt_ref = refs.pop(0)
    txt_ref = refs.pop(0) if first else txt_in
    acc_ref, lr_ref, lc_ref, turn_ref, *more = refs
    x_refs, xt_refs, e_refs, r_refs, c_refs = [more[count * i : count * (i + 1)] for i in range(5)]
    rows = img_refs[0].shape[0] - EXTRA
    cols, dim = txt_ref.shape
    texts = cols // txt_tok
    steps = cols // chunk
    groups = rows // 8
    every = range(0, cols, chunk)

    def lanes(x):
        return [x[:, 128 * i : 128 * (i + 1)] for i in range(x.shape[1] // 128)]

    def fold_rows(x, op):
        return op(x.reshape(2, groups, 8, x.shape[1]), axis=1)

    def spread(x):
        return jnp.broadcast_to(x[:, None], (2, groups) + x.shape[1:]).reshape(2 * rows, x.shape[2])

    def over_lanes(x, op):
        shift = 64
        while shift >= texts:
            x = op(x, pltpu.roll(x, shift, x.ndim - 1))
            shift //= 2
        return x

    def over_rows(x, op):
        return op(x, pltpu.roll(x, 4, 1))

    def over_tokens(x):
        return over_lanes(sum(x[:, :, 128 * i : 128 * (i + 1)] for i in range(cols // 128)), jnp.add)

    def scores(p, at):
        return lax.dot_general(
            x_refs[p][...], txt_ref[pl.ds(at, chunk), :], (((1,), (1,)), ((), ())), preferred_element_type=jnp.float32
        )

    def verdicts(p, row_lse_sum, col_lse_sum):
        logits = LOGIT_SCALE * (row_lse_sum * (0.5 / img_tok) + col_lse_sum * (0.5 / txt_tok)) + LOGIT_BIAS
        positives = jnp.stack([img_refs[2 * p + b][rows:, :128].astype(jnp.float32)[:8] for b in range(2)])
        sign = jnp.where(ids_ref[...][None] == positives, 1.0, -1.0).astype(jnp.float32)
        z = -sign * logits
        slope = -sign * (SCORE_SCALE * LOGIT_SCALE) / (1.0 + jnp.exp(-z))
        loss = jnp.maximum(z, 0.0) + jnp.log1p(jnp.exp(-jnp.abs(z)))
        loss = jnp.sum(loss, axis=2, keepdims=True) * (texts / 128)
        coarse = loss.astype(jnp.bfloat16).astype(jnp.float32)
        part = jnp.where(lax.broadcasted_iota(jnp.int32, (2, 8, 1), 1) < 4, coarse, loss - coarse)
        none = jnp.zeros_like(part[0])
        for b, found in enumerate(([part[0], none], [none, part[1]])):
            gi_ref = gi_refs[2 * p + b]
            gi_ref[rows:] = jnp.broadcast_to(jnp.concatenate(found, axis=0), (EXTRA, dim)).astype(gi_ref.dtype)
        return slope

    def weights(p, at, width):
        parts = []
        for i in range(width // 128):
            e = e_refs[p][:, pl.ds(at + 128 * i, 128)].reshape(2, groups, 8, 128)
            factor = r_refs[p][...].reshape(2, groups, 8, 128) + c_refs[p][:, :, pl.ds(at + 128 * i, 128)][:, None]
            parts.append((e * factor).reshape(2 * rows, 128).astype(jnp.bfloat16))
        return jnp.concatenate(parts, axis=1)

    def store_image_grad(p, grad):
        for b in range(2):
            gi_ref = gi_refs[2 * p + b]
            gi_ref[:rows] = grad[b * rows : (b + 1) * rows].astype(gi_ref.dtype)

    def fast_scores(p):
        for at in every:
            e = jnp.exp2(scores(p, at) * (SCORE_SCALE * LOG2E))
            e_refs[p][:, at : at + chunk] = e
            part = functools.reduce(jnp.add, lanes(e))
            r_refs[p][...] = part if at == 0 else r_refs[p][...] + part
            c_refs[p][:, :, at : at + chunk] = fold_rows(e, jnp.sum)

    def fast_factors(p):
        row_log = jnp.log2(over_lanes(r_refs[p][...], jnp.add))
        col_log = jnp.log2(over_rows(c_refs[p][...], jnp.add))
        low = jnp.minimum(jnp.min(fold_rows(row_log, jnp.min)), jnp.min(col_log))
        high = jnp.maximum(jnp.max(fold_rows(row_log, jnp.max)), jnp.max(col_log))
        row_lse = over_rows(fold_rows(row_log, jnp.sum), jnp.add)
        slope = verdicts(p, row_lse * (1.0 / LOG2E), over_tokens(col_log) * (1.0 / LOG2E))
        r_refs[p][...] = spread(slope * (0.5 / img_tok)) * jnp.exp2(-row_log)
        c_refs[p][...] = jnp.concatenate([slope * (0.5 / txt_tok)] * (cols // 128), axis=2) * jnp.exp2(-col_log)
        return jnp.logical_and(low > -100.0, high < 100.0)

    def fast_gradients(p):
        grad = None
        for at in range(0, cols, 256):
            w = weights(p, at, 256)
            part = jnp.dot(w, txt_ref[at : at + 256, :], preferred_element_type=jnp.float32)
            grad = part if grad is None else grad + part
            part = jnp.dot(xt_refs[p][...], w, preferred_element_type=jnp.float32)
            acc_ref[:, at : at + 256] = part if p == 0 else acc_ref[:, at : at + 256] + part
        store_image_grad(p, grad)

    def slow_pair(p):
        e_ref, r_ref, c_ref = e_refs[p], r_refs[p], c_refs[p]
        r_ref[...] = jnp.full_like(r_ref, -jnp.inf)

        def tops(j, carry):
            at = pl.multiple_of(j * chunk, chunk)
            s = SCORE_SCALE * scores(p, at)
            e_ref[:, pl.ds(at, chunk)] = s
            r_ref[...] = functools.reduce(jnp.maximum, lanes(s) + [r_ref[...]])
            c_ref[:, :, pl.ds(at, chunk)] = fold_rows(s, jnp.max)
            return carry

        lax.fori_loop(0, steps, tops, 0)
        r_ref[...] = over_lanes(r_ref[...], jnp.maximum)
        c_ref[...] = over_rows(c_ref[...], jnp.maximum)
        lr_ref[...] = jnp.zeros_like(lr_ref)

        def sums(j, carry):
            at = pl.multiple_of(j * 128, 128)
            s = e_ref[:, pl.ds(at, 128)]
            lr_ref[...] += jnp.exp(s - r_ref[...])
            lc_ref[:, :, pl.ds(at, 128)] = fold_rows(jnp.exp(s - spread(c_ref[:, :, pl.ds(at, 128)])), jnp.sum)
            return carry

        lax.fori_loop(0, cols // 128, sums, 0)
        lr_ref[...] = r_ref[...] + jnp.log(over_lanes(lr_ref[...], jnp.add))
        lc_ref[...] = c_ref[...] + jnp.log(over_rows(lc_ref[...], jnp.add))

        def mixtures(j, carry):
            at = pl.multiple_of(j * 128, 128)
            s = e_ref[:, pl.ds(at, 128)]
            by_col = jnp.exp(s - spread(lc_ref[:, :, pl.ds(at, 128)]))
            e_ref[:, pl.ds(at, 128)] = jnp.exp(s - lr_ref[...]) * (0.5 / img_tok) + by_col * (0.5 / txt_tok)
            return carry

        lax.fori_loop(0, cols // 128, mixtures, 0)
        slope = verdicts(p, over_rows(fold_rows(lr_ref[...], jnp.sum), jnp.add), over_tokens(lc_ref[...]))
        r_ref[...] = spread(slope)
        c_ref[...] = jnp.zeros_like(c_ref)

        def gradients(j, grad):
            at = pl.multiple_of(j * 256, 256)
            w = weights(p, at, 256)
            acc_ref[:, pl.ds(at, 256)] += jnp.dot(xt_refs[p][...], w, preferred_element_type=jnp.float32)
            return grad + jnp.dot(w, txt_ref[pl.ds(at, 256), :], preferred_element_type=jnp.float32)

        store_image_grad(p, lax.fori_loop(0, cols // 256, gradients, jnp.zeros((2 * rows, dim), jnp.float32)))

    if first:
        for h, part in enumerate(lanes(txt_in[...].astype(jnp.float32))):
            turn_ref[h] = part
        for q in range(txt_tok):
            picked = [turn_ref[h, pl.ds(q, texts, stride=txt_tok), :] for h in range(dim // 128)]
            txt_ref[q * texts : (q + 1) * texts, :] = jnp.concatenate(picked, axis=1).astype(jnp.bfloat16)
    for p in range(count):
        for b in range(2):
            x_refs[p][b * rows : (b + 1) * rows] = img_refs[2 * p + b][:rows]
        xt_refs[p][...] = x_refs[p][...].T
    safe = None
    for p in range(count + 1):
        if p < count:
            fast_scores(p)
        if p > 0:
            fine = fast_factors(p - 1)
            safe = fine if safe is None else jnp.logical_and(safe, fine)
            fast_gradients(p - 1)

    @pl.when(jnp.logical_not(safe))
    def _():
        acc_ref[...] = jnp.zeros_like(acc_ref)
        for p in range(count):
            slow_pair(p)

    total = acc_ref[...] if first else acc_ref[...] + gin_ref[...]
    if last:
        row = lax.broadcasted_iota(jnp.int32, (cols, 1), 0)
        source = (row % txt_tok) * texts + row // txt_tok
        pick = jnp.where(lax.broadcasted_iota(jnp.int32, (cols, cols), 1) == source, 1.0, 0.0).astype(gt_ref.dtype)
        gt_ref[...] = lax.dot_general(
            pick, total.astype(gt_ref.dtype), (((1,), (1,)), ((), ())), preferred_element_type=jnp.float32
        ).astype(gt_ref.dtype)
    else:
        gt_ref[...] = total


def pair_call(images, texts, ids, carried, img_tok, txt_tok, last, chunk=CHUNK):
    tall, dim = images[0].shape
    count = len(images) // 2
    rows = tall - EXTRA
    cols = texts.shape[0]
    first = carried is None
    out_shape = [jax.ShapeDtypeStruct((tall, dim), jnp.bfloat16 if b % 2 else jnp.float32) for b in range(2 * count)]
    out_shape.append(
        jax.ShapeDtypeStruct((cols, dim), jnp.bfloat16) if last else jax.ShapeDtypeStruct((dim, cols), jnp.float32)
    )
    if first:
        out_shape.append(jax.ShapeDtypeStruct((cols, dim), jnp.bfloat16))
    scratch = [
        pltpu.VMEM((dim, cols), jnp.float32),
        pltpu.VMEM((2 * rows, 128), jnp.float32),
        pltpu.VMEM((2, 8, cols), jnp.float32),
        pltpu.VMEM((dim // 128, cols, 128), jnp.float32),
    ]
    scratch += [pltpu.VMEM((2 * rows, dim), jnp.bfloat16)] * count
    scratch += [pltpu.VMEM((dim, 2 * rows), jnp.bfloat16)] * count
    scratch += [pltpu.VMEM((2 * rows, cols), jnp.float32)] * count
    scratch += [pltpu.VMEM((2 * rows, 128), jnp.float32)] * count
    scratch += [pltpu.VMEM((2, 8, cols), jnp.float32)] * count
    operands = [*images, texts, ids] + ([] if first else [carried])
    return pl.pallas_call(
        functools.partial(
            pair_kernel, count=count, chunk=chunk, img_tok=img_tok, txt_tok=txt_tok, first=first, last=last
        ),
        out_shape=out_shape,
        scratch_shapes=scratch,
        compiler_params=pltpu.CompilerParams(vmem_limit_bytes=(22 + 12 * (count - 1)) * 2**20),
    )(*operands)


def body(image_tokens, text_tokens, positives):
    devices = lax.axis_size(AXES)
    own_images, img_tok, dim = image_tokens.shape
    own_texts, txt_tok, _ = text_tokens.shape
    rows = own_images * img_tok
    place = lax.axis_index("blk") * lax.axis_size("grp") + lax.axis_index("grp")
    classes = sorted({i & CLASS for i in range(devices)})
    across_texts = [[i for i in range(devices) if i & CLASS == k] for k in classes]
    peers = len(across_texts[0])

    def swapped(x, bits):
        return lax.ppermute(x, AXES, [(i, i ^ bits) for i in range(devices)])

    labels = jnp.broadcast_to(jnp.tile(positives.astype(jnp.bfloat16), EXTRA // own_images)[:, None], (EXTRA, dim))
    own = jnp.concatenate([image_tokens.transpose(1, 0, 2).reshape(rows, dim), labels], axis=0)
    over = {bits: swapped(own, bits) for bits in (X_LOW, X_LOW | X_HIGH)}
    over[X_HIGH] = swapped(over[X_LOW], X_LOW | X_HIGH)

    sent = jnp.broadcast_to(text_tokens[None], (peers, own_texts, txt_tok, dim))
    texts = lax.all_to_all(sent, AXES, 0, 0, tiled=True, axis_index_groups=across_texts)
    X_BOTH = X_LOW | X_HIGH
    over[0] = own
    beside = {bits: swapped(x, CORE) for bits, x in over.items()}
    texts = texts.reshape(peers * own_texts * txt_tok, dim)
    lane = jnp.arange(128, dtype=jnp.int32) % (peers * own_texts)
    ids = ((lane // own_texts) * 4 + (place & CLASS)) * own_texts + lane % own_texts
    ids = jnp.broadcast_to(ids.astype(jnp.float32)[None], (8, 128))

    def summed(near, met):
        return (near + met.astype(jnp.float32)).astype(jnp.bfloat16)

    found, gathered = {}, None

    def work(pairs, last=False):
        nonlocal gathered, texts
        images = [x[bits] for bits in pairs for x in (over, beside)]
        out = pair_call(images, texts, ids, gathered, img_tok, txt_tok, last)
        texts = texts if gathered is not None else out[-1]
        gathered = out[len(images)]
        return out[: len(images)]

    out = work([X_LOW, X_BOTH])
    found[X_LOW] = (out[0], swapped(out[1], CORE))
    found[X_BOTH] = (out[2], swapped(out[3], CORE))
    *sent, gathered = lax.optimization_barrier((summed(*found[X_LOW]), summed(*found[X_BOTH]), gathered))
    back = [swapped(sent[0], X_LOW), swapped(sent[1], X_BOTH)]
    near, far = work([X_HIGH])
    met = swapped(far, CORE)
    out = work([0], last=True)
    back, near = lax.optimization_barrier((back, near))
    found[X_HIGH] = (near, met)
    met, gathered = lax.optimization_barrier((swapped(out[1], CORE), gathered))
    found[0] = (out[0], met)
    back.append(swapped(summed(*found[X_HIGH]), X_HIGH))

    grad = found[0][0] + found[0][1].astype(jnp.float32)
    for part in back:
        grad = grad + part.astype(jnp.float32)
    grad_image = grad[:rows].reshape(img_tok, own_images, dim).transpose(1, 0, 2)
    row_loss = sum(grad[rows + n : rows + n + own_images, 0] for n in range(0, EXTRA, own_images))

    sent = gathered.reshape(peers, own_texts, txt_tok, dim)
    parts = lax.all_to_all(sent, AXES, 0, 0, tiled=True, axis_index_groups=across_texts)
    grad_text = jnp.sum(parts.astype(jnp.float32), axis=0)
    return (row_loss, grad_image, grad_text)


def solution(mesh):
    placed = (P(AXES, None, None), P(AXES, None, None), P(AXES))
    return jax.shard_map(
        body,
        mesh=mesh,
        in_specs=placed,
        out_specs=(P(AXES), P(AXES, None, None), P(AXES, None, None)),
        check_vma=False,
    )
```

```python
import functools
import jax
import jax.numpy as jnp
from jax import lax
from jax.experimental import pallas as pl
from jax.experimental.pallas import tpu as pltpu
from jax.sharding import PartitionSpec as P

SCORE_SCALE = 16.0
LOGIT_SCALE = 4.0
LOGIT_BIAS = -25.5
LOG2E = 1.4426950408889634
EXTRA = 16
CHUNK = 256
AXES = ("blk", "grp")
CORE, X_LOW, X_HIGH = 1, 2, 64
CLASS = CORE | X_LOW | X_HIGH


def pair_kernel(*refs, count, chunk, img_tok, txt_tok, first, last):
    refs = list(refs)
    img_refs = [refs.pop(0) for _ in range(2 * count)]
    txt_in, ids_ref = refs.pop(0), refs.pop(0)
    gin_ref = None if first else refs.pop(0)
    gi_refs = [refs.pop(0) for _ in range(2 * count)]
    gt_ref = refs.pop(0)
    txt_ref = refs.pop(0) if first else txt_in
    acc_ref, lr_ref, lc_ref, turn_ref, *more = refs
    x_refs, xt_refs, e_refs, r_refs, c_refs = [more[count * i : count * (i + 1)] for i in range(5)]
    rows = img_refs[0].shape[0] - EXTRA
    cols, dim = txt_ref.shape
    texts = cols // txt_tok
    steps = cols // chunk
    groups = rows // 8
    every = range(0, cols, chunk)

    def lanes(x):
        return [x[:, 128 * i : 128 * (i + 1)] for i in range(x.shape[1] // 128)]

    def fold_rows(x, op):
        return op(x.reshape(2, groups, 8, x.shape[1]), axis=1)

    def spread(x):
        return jnp.broadcast_to(x[:, None], (2, groups) + x.shape[1:]).reshape(2 * rows, x.shape[2])

    def over_lanes(x, op):
        shift = 64
        while shift >= texts:
            x = op(x, pltpu.roll(x, shift, x.ndim - 1))
            shift //= 2
        return x

    def over_rows(x, op):
        return op(x, pltpu.roll(x, 4, 1))

    def over_tokens(x):
        return over_lanes(sum(x[:, :, 128 * i : 128 * (i + 1)] for i in range(cols // 128)), jnp.add)

    def scores(p, at):
        return lax.dot_general(
            x_refs[p][...], txt_ref[pl.ds(at, chunk), :], (((1,), (1,)), ((), ())), preferred_element_type=jnp.float32
        )

    def verdicts(p, row_lse_sum, col_lse_sum):
        logits = LOGIT_SCALE * (row_lse_sum * (0.5 / img_tok) + col_lse_sum * (0.5 / txt_tok)) + LOGIT_BIAS
        positives = jnp.stack([img_refs[2 * p + b][rows:, :128].astype(jnp.float32)[:8] for b in range(2)])
        sign = jnp.where(ids_ref[...][None] == positives, 1.0, -1.0).astype(jnp.float32)
        z = -sign * logits
        slope = -sign * (SCORE_SCALE * LOGIT_SCALE) / (1.0 + jnp.exp(-z))
        loss = jnp.maximum(z, 0.0) + jnp.log1p(jnp.exp(-jnp.abs(z)))
        loss = jnp.sum(loss, axis=2, keepdims=True) * (texts / 128)
        coarse = loss.astype(jnp.bfloat16).astype(jnp.float32)
        part = jnp.where(lax.broadcasted_iota(jnp.int32, (2, 8, 1), 1) < 4, coarse, loss - coarse)
        none = jnp.zeros_like(part[0])
        for b, found in enumerate(([part[0], none], [none, part[1]])):
            gi_ref = gi_refs[2 * p + b]
            gi_ref[rows:] = jnp.broadcast_to(jnp.concatenate(found, axis=0), (EXTRA, dim)).astype(gi_ref.dtype)
        return slope

    def weights(p, at, width):
        parts = []
        for i in range(width // 128):
            e = e_refs[p][:, pl.ds(at + 128 * i, 128)].reshape(2, groups, 8, 128)
            factor = r_refs[p][...].reshape(2, groups, 8, 128) + c_refs[p][:, :, pl.ds(at + 128 * i, 128)][:, None]
            parts.append((e * factor).reshape(2 * rows, 128).astype(jnp.bfloat16))
        return jnp.concatenate(parts, axis=1)

    def store_image_grad(p, grad):
        for b in range(2):
            gi_ref = gi_refs[2 * p + b]
            gi_ref[:rows] = grad[b * rows : (b + 1) * rows].astype(gi_ref.dtype)

    def fast_scores(p):
        for at in every:
            e = jnp.exp2(scores(p, at) * (SCORE_SCALE * LOG2E))
            e_refs[p][:, at : at + chunk] = e
            part = functools.reduce(jnp.add, lanes(e))
            r_refs[p][...] = part if at == 0 else r_refs[p][...] + part
            c_refs[p][:, :, at : at + chunk] = fold_rows(e, jnp.sum)

    def fast_factors(p):
        row_log = jnp.log2(over_lanes(r_refs[p][...], jnp.add))
        col_log = jnp.log2(over_rows(c_refs[p][...], jnp.add))
        low = jnp.minimum(jnp.min(fold_rows(row_log, jnp.min)), jnp.min(col_log))
        high = jnp.maximum(jnp.max(fold_rows(row_log, jnp.max)), jnp.max(col_log))
        row_lse = over_rows(fold_rows(row_log, jnp.sum), jnp.add)
        slope = verdicts(p, row_lse * (1.0 / LOG2E), over_tokens(col_log) * (1.0 / LOG2E))
        r_refs[p][...] = spread(slope * (0.5 / img_tok)) * jnp.exp2(-row_log)
        c_refs[p][...] = jnp.concatenate([slope * (0.5 / txt_tok)] * (cols // 128), axis=2) * jnp.exp2(-col_log)
        return jnp.logical_and(low > -100.0, high < 100.0)

    def fast_gradients(p):
        grad = None
        for at in range(0, cols, 256):
            w = weights(p, at, 256)
            part = jnp.dot(w, txt_ref[at : at + 256, :], preferred_element_type=jnp.float32)
            grad = part if grad is None else grad + part
            part = jnp.dot(xt_refs[p][...], w, preferred_element_type=jnp.float32)
            acc_ref[:, at : at + 256] = part if p == 0 else acc_ref[:, at : at + 256] + part
        store_image_grad(p, grad)

    def slow_pair(p):
        e_ref, r_ref, c_ref = e_refs[p], r_refs[p], c_refs[p]
        r_ref[...] = jnp.full_like(r_ref, -jnp.inf)

        def tops(j, carry):
            at = pl.multiple_of(j * chunk, chunk)
            s = SCORE_SCALE * scores(p, at)
            e_ref[:, pl.ds(at, chunk)] = s
            r_ref[...] = functools.reduce(jnp.maximum, lanes(s) + [r_ref[...]])
            c_ref[:, :, pl.ds(at, chunk)] = fold_rows(s, jnp.max)
            return carry

        lax.fori_loop(0, steps, tops, 0)
        r_ref[...] = over_lanes(r_ref[...], jnp.maximum)
        c_ref[...] = over_rows(c_ref[...], jnp.maximum)
        lr_ref[...] = jnp.zeros_like(lr_ref)

        def sums(j, carry):
            at = pl.multiple_of(j * 128, 128)
            s = e_ref[:, pl.ds(at, 128)]
            lr_ref[...] += jnp.exp(s - r_ref[...])
            lc_ref[:, :, pl.ds(at, 128)] = fold_rows(jnp.exp(s - spread(c_ref[:, :, pl.ds(at, 128)])), jnp.sum)
            return carry

        lax.fori_loop(0, cols // 128, sums, 0)
        lr_ref[...] = r_ref[...] + jnp.log(over_lanes(lr_ref[...], jnp.add))
        lc_ref[...] = c_ref[...] + jnp.log(over_rows(lc_ref[...], jnp.add))

        def mixtures(j, carry):
            at = pl.multiple_of(j * 128, 128)
            s = e_ref[:, pl.ds(at, 128)]
            by_col = jnp.exp(s - spread(lc_ref[:, :, pl.ds(at, 128)]))
            e_ref[:, pl.ds(at, 128)] = jnp.exp(s - lr_ref[...]) * (0.5 / img_tok) + by_col * (0.5 / txt_tok)
            return carry

        lax.fori_loop(0, cols // 128, mixtures, 0)
        slope = verdicts(p, over_rows(fold_rows(lr_ref[...], jnp.sum), jnp.add), over_tokens(lc_ref[...]))
        r_ref[...] = spread(slope)
        c_ref[...] = jnp.zeros_like(c_ref)

        def gradients(j, grad):
            at = pl.multiple_of(j * 256, 256)
            w = weights(p, at, 256)
            acc_ref[:, pl.ds(at, 256)] += jnp.dot(xt_refs[p][...], w, preferred_element_type=jnp.float32)
            return grad + jnp.dot(w, txt_ref[pl.ds(at, 256), :], preferred_element_type=jnp.float32)

        store_image_grad(p, lax.fori_loop(0, cols // 256, gradients, jnp.zeros((2 * rows, dim), jnp.float32)))

    if first:
        for h, part in enumerate(lanes(txt_in[...].astype(jnp.float32))):
            turn_ref[h] = part
        for q in range(txt_tok):
            picked = [turn_ref[h, pl.ds(q, texts, stride=txt_tok), :] for h in range(dim // 128)]
            txt_ref[q * texts : (q + 1) * texts, :] = jnp.concatenate(picked, axis=1).astype(jnp.bfloat16)
    for p in range(count):
        for b in range(2):
            x_refs[p][b * rows : (b + 1) * rows] = img_refs[2 * p + b][:rows]
        xt_refs[p][...] = x_refs[p][...].T
    safe = None
    for p in range(count + 1):
        if p < count:
            fast_scores(p)
        if p > 0:
            fine = fast_factors(p - 1)
            safe = fine if safe is None else jnp.logical_and(safe, fine)
            fast_gradients(p - 1)

    @pl.when(jnp.logical_not(safe))
    def _():
        acc_ref[...] = jnp.zeros_like(acc_ref)
        for p in range(count):
            slow_pair(p)

    total = acc_ref[...] if first else acc_ref[...] + gin_ref[...]
    if last:
        row = lax.broadcasted_iota(jnp.int32, (cols, 1), 0)
        source = (row % txt_tok) * texts + row // txt_tok
        pick = jnp.where(lax.broadcasted_iota(jnp.int32, (cols, cols), 1) == source, 1.0, 0.0).astype(gt_ref.dtype)
        gt_ref[...] = lax.dot_general(
            pick, total.astype(gt_ref.dtype), (((1,), (1,)), ((), ())), preferred_element_type=jnp.float32
        ).astype(gt_ref.dtype)
    else:
        gt_ref[...] = total


def pair_call(images, texts, ids, carried, img_tok, txt_tok, last, chunk=CHUNK):
    tall, dim = images[0].shape
    count = len(images) // 2
    rows = tall - EXTRA
    cols = texts.shape[0]
    first = carried is None
    out_shape = [jax.ShapeDtypeStruct((tall, dim), jnp.bfloat16 if b % 2 else jnp.float32) for b in range(2 * count)]
    out_shape.append(
        jax.ShapeDtypeStruct((cols, dim), jnp.bfloat16) if last else jax.ShapeDtypeStruct((dim, cols), jnp.float32)
    )
    if first:
        out_shape.append(jax.ShapeDtypeStruct((cols, dim), jnp.bfloat16))
    scratch = [
        pltpu.VMEM((dim, cols), jnp.float32),
        pltpu.VMEM((2 * rows, 128), jnp.float32),
        pltpu.VMEM((2, 8, cols), jnp.float32),
        pltpu.VMEM((dim // 128, cols, 128), jnp.float32),
    ]
    scratch += [pltpu.VMEM((2 * rows, dim), jnp.bfloat16)] * count
    scratch += [pltpu.VMEM((dim, 2 * rows), jnp.bfloat16)] * count
    scratch += [pltpu.VMEM((2 * rows, cols), jnp.float32)] * count
    scratch += [pltpu.VMEM((2 * rows, 128), jnp.float32)] * count
    scratch += [pltpu.VMEM((2, 8, cols), jnp.float32)] * count
    operands = [*images, texts, ids] + ([] if first else [carried])
    return pl.pallas_call(
        functools.partial(
            pair_kernel, count=count, chunk=chunk, img_tok=img_tok, txt_tok=txt_tok, first=first, last=last
        ),
        out_shape=out_shape,
        scratch_shapes=scratch,
        compiler_params=pltpu.CompilerParams(vmem_limit_bytes=(17 + 11 * (count - 1)) * 2**20),
    )(*operands)


def body(image_tokens, text_tokens, positives):
    devices = lax.axis_size(AXES)
    own_images, img_tok, dim = image_tokens.shape
    own_texts, txt_tok, _ = text_tokens.shape
    rows = own_images * img_tok
    place = lax.axis_index("blk") * lax.axis_size("grp") + lax.axis_index("grp")
    classes = sorted({i & CLASS for i in range(devices)})
    across_texts = [[i for i in range(devices) if i & CLASS == k] for k in classes]
    peers = len(across_texts[0])

    def swapped(x, bits):
        return lax.ppermute(x, AXES, [(i, i ^ bits) for i in range(devices)])

    labels = jnp.broadcast_to(jnp.tile(positives.astype(jnp.bfloat16), EXTRA // own_images)[:, None], (EXTRA, dim))
    own = jnp.concatenate([image_tokens.transpose(1, 0, 2).reshape(rows, dim), labels], axis=0)
    over = {bits: swapped(own, bits) for bits in (X_LOW, X_LOW | X_HIGH)}
    over[X_HIGH] = swapped(over[X_LOW], X_LOW | X_HIGH)

    sent = jnp.broadcast_to(text_tokens[None], (peers, own_texts, txt_tok, dim))
    texts = lax.all_to_all(sent, AXES, 0, 0, tiled=True, axis_index_groups=across_texts)
    X_BOTH = X_LOW | X_HIGH
    over[0] = own
    beside = {bits: swapped(x, CORE) for bits, x in over.items()}
    texts = texts.reshape(peers * own_texts * txt_tok, dim)
    lane = jnp.arange(128, dtype=jnp.int32) % (peers * own_texts)
    ids = ((lane // own_texts) * 4 + (place & CLASS)) * own_texts + lane % own_texts
    ids = jnp.broadcast_to(ids.astype(jnp.float32)[None], (8, 128))

    def summed(near, met):
        return (near + met.astype(jnp.float32)).astype(jnp.bfloat16)

    found, gathered = {}, None

    def work(pairs, last=False):
        nonlocal gathered, texts
        images = [x[bits] for bits in pairs for x in (over, beside)]
        out = pair_call(images, texts, ids, gathered, img_tok, txt_tok, last)
        texts = texts if gathered is not None else out[-1]
        gathered = out[len(images)]
        return out[: len(images)]

    out = work([X_LOW, X_BOTH])
    found[X_LOW] = (out[0], swapped(out[1], CORE))
    found[X_BOTH] = (out[2], swapped(out[3], CORE))
    *sent, gathered = lax.optimization_barrier((summed(*found[X_LOW]), summed(*found[X_BOTH]), gathered))
    back = [swapped(sent[0], X_LOW), swapped(sent[1], X_BOTH)]
    near, far = work([X_HIGH])
    met = swapped(far, CORE)
    out = work([0], last=True)
    back, near = lax.optimization_barrier((back, near))
    found[X_HIGH] = (near, met)
    met, gathered = lax.optimization_barrier((swapped(out[1], CORE), gathered))
    found[0] = (out[0], met)
    back.append(swapped(summed(*found[X_HIGH]), X_HIGH))

    grad = found[0][0] + found[0][1].astype(jnp.float32)
    for part in back:
        grad = grad + part.astype(jnp.float32)
    grad_image = grad[:rows].reshape(img_tok, own_images, dim).transpose(1, 0, 2)
    row_loss = sum(grad[rows + n : rows + n + own_images, 0] for n in range(0, EXTRA, own_images))

    sent = gathered.reshape(peers, own_texts, txt_tok, dim)
    parts = lax.all_to_all(sent, AXES, 0, 0, tiled=True, axis_index_groups=across_texts)
    grad_text = jnp.sum(parts.astype(jnp.float32), axis=0)
    return (row_loss, grad_image, grad_text)


def solution(mesh):
    placed = (P(AXES, None, None), P(AXES, None, None), P(AXES))
    return jax.shard_map(
        body,
        mesh=mesh,
        in_specs=placed,
        out_specs=(P(AXES), P(AXES, None, None), P(AXES, None, None)),
        check_vma=False,
    )
```
